256 devices in a mesh: rep: 8 (over z), exp: 32 (over y, x, core).
Axes of the slice: x: 4, y: 4, z: 8, core: 2. Of those that a mesh axis runs over, the one named last changes fastest.
Arguments:
- tokens: bfloat16 [12288, 2048], P(('rep', 'exp')), may hold values from -6 to 6
- grad_out: bfloat16 [12288, 2048], P(('rep', 'exp')), may hold values from -6 to 6
- expert_ids: int32 [12288, 8], P(('rep', 'exp')), may hold values from 0 to 127, all different within a row; in each aligned block of 48 rows (0 to 47, 48 to 95, ...) at most 4 rows name the same one
- gate_probs: float32 [12288, 8], P(('rep', 'exp')), may hold values from 0.05 to 1
- gate_weight: bfloat16 [256, 2048, 384], P(('rep', 'exp')), may hold values from -0.125 to 0.125
- up_weight: bfloat16 [256, 2048, 384], P(('rep', 'exp')), may hold values from -0.125 to 0.125
- down_weight: bfloat16 [256, 384, 2048], P(('rep', 'exp')), may hold values from -0.21875 to 0.21875
Outputs:
- token_grad: bfloat16 [12288, 2048], P(('rep', 'exp'))
- gate_grad: bfloat16 [256, 2048, 384], P(('rep', 'exp'))
- up_grad: bfloat16 [256, 2048, 384], P(('rep', 'exp'))
- down_grad: bfloat16 [256, 384, 2048], P(('rep', 'exp'))
The draws below stay inside these ranges and needn't reach their ends.
Inputs may be any that keep to these rules, and one draw needn't show every extreme that they name: `expert_ids`: the 8 experts of a token are distinct; among the 48 tokens of one device no expert is chosen more than 4 times, and that many in some device.
All inputs are finite; a program needn't handle non-finite values.
Results may differ from the reference program's by a relative error of at most 0.0058.
Values may be sent and summed in bfloat16 or wider, within the bound.
A program may use at most 128 MiB of HBM per device.

```python
import math
import jax
import jax.numpy as jnp
import numpy as np
from jax import lax

D = 2048
FF = 768
TOP = 8
TOK_DEV = 48
EXPERTS = 128
CAP = 4
TOKENS = 12288
SLOTS = 1024


def block_scale(key, extent, split, low, top_value):
    gain = 1.0
    for dim, shards_of in split:
        steps = jax.random.uniform(jax.random.fold_in(jax.random.fold_in(key, 6), dim), (shards_of,), jnp.float32, low / len(split), top_value / len(split))
        gain = gain * jnp.repeat(jnp.exp(steps), extent[dim] // shards_of).reshape((-1,) + (1,) * (len(extent) - 1 - dim))
    return gain


def routed_block(key, own, number, rows, count, top, reach, slope):
    order = jax.random.permutation(key, count)
    heavy_load, common = portions_of(count, rows * top, reach, slope, True), portions_of(count, rows * top, reach, slope, False)
    places = jnp.arange(count)

    def named(lengths, turn):
        used = int((lengths > 0).sum())
        fixed = max(1, used // 4)
        shifted = fixed + (places - fixed + turn * (used - fixed)) % max(1, count - fixed)
        return jnp.zeros((count,), jnp.int32).at[order[jnp.where(places < fixed, places, shifted)]].set(jnp.asarray(lengths, jnp.int32))

    lengths = jnp.where(number % 4 == 0, named(heavy_load, number // 4), named(common, number - number // 4 - 1))
    mixed = jax.random.permutation(jax.random.fold_in(own, 3), count)
    donor, sink = mixed[0:count // 2 * 2:2], mixed[1:count // 2 * 2:2]
    margin = jnp.minimum(lengths[donor] - 1, reach - lengths[sink]) // 2
    margin = jnp.where((donor == order[0]) | (sink == order[0]) | (lengths[sink] == 0), 0, jnp.maximum(margin, 0))
    shifted = jax.random.randint(jax.random.fold_in(own, 4), (count // 2,), 0, 1 << 20) % (margin + 1)
    lengths = lengths.at[donor].add(-shifted).at[sink].add(shifted)
    members = jnp.searchsorted(jnp.cumsum(lengths), jnp.arange(rows * top), side="right").astype(jnp.int32)
    table = members.reshape(top, rows).T
    table = table[jax.random.permutation(jax.random.fold_in(own, 1), rows)]
    turn = jax.random.randint(jax.random.fold_in(own, 2), (rows, 1), 0, top)
    return jnp.take_along_axis(table, (jnp.arange(top)[None, :] + turn) % top, axis=1)


def portions_of(count, total, bound, lean, full):
    loads = [(1 << 20) // math.isqrt(rank ** lean) + 1 for rank in range(1, count + 1)]
    largest = bound if full else min(bound, max(-(-total // count), total * loads[0] // sum(loads)))
    least = 1 if total - largest >= count - 1 else 0
    counts, spare = [largest] + [least] * (count - 1), total - largest - least * (count - 1)
    while spare > 0:
        free = [i for i in range(1, count) if counts[i] < largest] or [i for i in range(1, count) if counts[i] < bound]
        pool, left = sum([loads[i] for i in free]), spare
        for i in free:
            extra = min(bound - counts[i], max(1, left * loads[i] // pool), spare)
            counts[i] = counts[i] + extra
            spare = spare - extra
    return np.array(counts)


def scatter_about(own_key, shape, width, bound, split=(), kind=jnp.bfloat16):
    drawn = jax.random.normal(own_key, shape, jnp.float32) * width
    if len(split) > 0:
        drawn = block_scale(own_key, shape, split, -0.22, 0.18) * drawn
    return jnp.clip(drawn, min=-bound, max=bound).astype(kind)


def setup_inputs(seed: int = 0) -> dict:
    splits = jax.random.split(jax.random.key(seed), 8)
    tokens = scatter_about(splits[0], (TOKENS, D), 1.0, 6.0, ((0, 256),))
    grad_out = scatter_about(splits[1], (TOKENS, D), 1.0, 6.0, ((0, 256),))
    expert_ids_keys = jax.random.split(jax.random.fold_in(splits[2], 1), TOKENS // TOK_DEV)
    expert_ids_turns = jax.random.permutation(jax.random.fold_in(splits[2], 3), TOKENS // TOK_DEV)
    expert_ids = jax.vmap(lambda own, number: routed_block(jax.random.fold_in(splits[2], 2), own, number, TOK_DEV, EXPERTS, TOP, CAP, 2))(expert_ids_keys, expert_ids_turns).reshape((TOKENS, TOP))
    gate_probs = jnp.clip(0.05 + 0.95 * jax.random.uniform(splits[3], (TOKENS, TOP), jnp.float32) ** block_scale(splits[3], (TOKENS, TOP), ((0, 256),), -0.2, 0.2), 0.05, 1.0)
    gate_weight = scatter_about(splits[4], (2 * EXPERTS, D, FF // 2), D ** -0.5, 0.125, ((0, 256),))
    up_weight = scatter_about(splits[5], (2 * EXPERTS, D, FF // 2), D ** -0.5, 0.125, ((0, 256),))
    down_weight = scatter_about(splits[6], (2 * EXPERTS, FF // 2, D), FF ** -0.5, 0.21875, ((0, 256),))
    return {"tokens": tokens, "grad_out": grad_out, "expert_ids": expert_ids, "gate_probs": gate_probs, "gate_weight": gate_weight, "up_weight": up_weight, "down_weight": down_weight}


def reference(tokens, grad_out, expert_ids, gate_probs, gate_weight, up_weight, down_weight):
    half = FF // 2
    gate_full = gate_weight.reshape(EXPERTS, 2, D, half).transpose(0, 2, 1, 3).reshape(EXPERTS, D, FF)
    up_full = up_weight.reshape(EXPERTS, 2, D, half).transpose(0, 2, 1, 3).reshape(EXPERTS, D, FF)
    down_full = down_weight.reshape(EXPERTS, FF, D)
    flat_ids = expert_ids.reshape(-1)
    flat_probs = gate_probs.reshape(-1)

    def expert_step(accumulated, inputs):
        expert_index, gate_mat, up_mat, down_mat = inputs
        matches = flat_ids == expert_index
        positions = jnp.nonzero(matches, size=SLOTS, fill_value=0)[0].astype(jnp.int32)
        match_count = jnp.sum(matches.astype(jnp.int32))
        validity = (jnp.arange(SLOTS, dtype=jnp.int32) < match_count).astype(jnp.float32)
        token_ids = (positions // TOP).astype(jnp.int32)
        rows_in = (tokens[token_ids].astype(jnp.float32) * validity[:, None]).astype(jnp.bfloat16)
        rows_grad = (flat_probs[positions][:, None] * grad_out[token_ids].astype(jnp.float32) * validity[:, None]).astype(jnp.bfloat16)
        gate_pre = jnp.dot(rows_in, gate_mat, preferred_element_type=jnp.float32)
        up_pre = jnp.dot(rows_in, up_mat, preferred_element_type=jnp.float32)
        sigmoid_gate = jax.nn.sigmoid(gate_pre)
        activated = gate_pre * sigmoid_gate
        hidden = (activated * up_pre).astype(jnp.bfloat16)
        hidden_grad = jnp.dot(rows_grad, down_mat.T, preferred_element_type=jnp.float32)
        up_in = (hidden_grad * activated).astype(jnp.bfloat16)
        gate_in = (hidden_grad * up_pre * sigmoid_gate * (1.0 + gate_pre * (1.0 - sigmoid_gate))).astype(jnp.bfloat16)
        contrib = jnp.dot(gate_in, gate_mat.T, preferred_element_type=jnp.float32) + jnp.dot(up_in, up_mat.T, preferred_element_type=jnp.float32)
        accumulated = accumulated.at[token_ids].add(contrib * validity[:, None])
        grad_gate = jnp.dot(rows_in.T, gate_in, preferred_element_type=jnp.float32).astype(jnp.bfloat16)
        grad_up = jnp.dot(rows_in.T, up_in, preferred_element_type=jnp.float32).astype(jnp.bfloat16)
        grad_down = jnp.dot(hidden.T, rows_grad, preferred_element_type=jnp.float32).astype(jnp.bfloat16)
        return accumulated, (grad_gate, grad_up, grad_down)

    start = jnp.zeros((TOKENS, D), jnp.float32)
    indices = jnp.arange(EXPERTS, dtype=jnp.int32)
    accumulated, stacked = lax.scan(expert_step, start, (indices, gate_full, up_full, down_full))
    grad_gate, grad_up, grad_down = stacked
    gate_grad = grad_gate.reshape(EXPERTS, D, 2, half).transpose(0, 2, 1, 3).reshape(2 * EXPERTS, D, half)
    up_grad = grad_up.reshape(EXPERTS, D, 2, half).transpose(0, 2, 1, 3).reshape(2 * EXPERTS, D, half)
    down_grad = grad_down.reshape(2 * EXPERTS, half, D)
    return (accumulated.astype(jnp.bfloat16), gate_grad, up_grad, down_grad)
```

```python
import jax
import jax.numpy as jnp
from jax import lax
from jax.experimental import pallas as pl
from jax.experimental.pallas import tpu as pltpu
from jax.sharding import PartitionSpec as P

MESH = pl.DeviceIdType.MESH
F32 = jnp.float32
BF16 = jnp.bfloat16
REP = 8
ROWS = 48
D = 2048
HALF = 384
TOP = 8
GROUPS = 4
NT = (((1,), (1,)), ((), ()))
TN = (((0,), (0,)), ((), ()))


UP = (0, 1, 3, 5, 7)
DOWN = (0, 2, 4, 6, 7)
OFFSET = (0, 7, 1, 6, 2, 5, 3, 4)


def kernel(
    tok_hbm, grad_hbm, meta_hbm, gate_hbm, up_hbm, down_hbm,
    tok_out, gate_out, up_out, down_out,
    tok, grad, meta, wgu, wd, send, recv, xs, gs, hid, giui, rsend, rrecv, selt,
    zsend, zrecv, own, gu_send, gu_recv, d_send, d_recv,
    load_sem, ring_s, ring_r, w_s, w_r, disp_s, disp_r, ret_s, ret_r, z_s, z_r, g_s, g_r,
):
    z = lax.axis_index("rep")
    e = lax.axis_index("exp")
    p = e // 2
    core = e % 2
    px = p % 4
    py = p // 4
    partner = (z, p * 2 + 1 - core)

    def plane(i):
        return ((py + i // 4) % 4) * 4 + (px + i % 4) % 4

    def zdev(d):
        return ((z + d) % REP, e)

    loads = [
        pltpu.make_async_copy(meta_hbm, meta.at[0], load_sem.at[0]),
        pltpu.make_async_copy(tok_hbm, tok.at[0], load_sem.at[1]),
        pltpu.make_async_copy(grad_hbm, grad.at[0], load_sem.at[2]),
        pltpu.make_async_copy(gate_hbm, wgu.at[:, pl.ds(0, HALF)], load_sem.at[3]),
        pltpu.make_async_copy(up_hbm, wgu.at[:, pl.ds(HALF, HALF)], load_sem.at[4]),
        pltpu.make_async_copy(down_hbm, wd.at[pl.ds(0, HALF)], load_sem.at[5]),
    ]
    for c in loads:
        c.start()

    barrier = pltpu.get_barrier_semaphore()

    def greet_plane(i, carry):
        pl.semaphore_signal(barrier, inc=1, device_id=(z, plane(i) * 2 + core), device_id_type=MESH)
        return carry

    def greet_z(i, carry):
        pl.semaphore_signal(barrier, inc=1, device_id=zdev(i), device_id_type=MESH)
        return carry

    lax.fori_loop(1, 16, greet_plane, 0)
    lax.fori_loop(1, REP, greet_z, 0)
    pl.semaphore_signal(barrier, inc=1, device_id=partner, device_id_type=MESH)
    pl.semaphore_wait(barrier, 23)

    def hop(direction, h, piece):
        table = (UP, DOWN)[direction]
        buf = (tok, grad, meta)[piece]
        return pltpu.make_async_remote_copy(
            src_ref=buf.at[table[h - 1]],
            dst_ref=buf.at[table[h]],
            send_sem=ring_s.at[direction, h - 1, piece],
            recv_sem=ring_r.at[direction, h - 1, piece],
            device_id=zdev((1, 7)[direction]),
            device_id_type=MESH,
        )

    def pieces(direction, h):
        if h < 4:
            return (2, 0, 1)
        return ((2, 0), (1,))[direction]

    for c in loads[:3]:
        c.wait()
    for piece in (2, 0, 1):
        for direction in (0, 1):
            hop(direction, 1, piece).start()

    def advance(h):
        for piece in (2, 0, 1):
            for direction in (0, 1):
                if piece in pieces(direction, h):
                    hop(direction, h, piece).wait_recv()
                    if h < 4 and piece in pieces(direction, h + 1):
                        hop(direction, h + 1, piece).start()

    def weight_copy(k):
        if k < 2:
            src = wgu.at[:, pl.ds(k * HALF, HALF)]
            dst = wgu.at[:, pl.ds((k + 2) * HALF, HALF)]
        else:
            src = wd.at[pl.ds(0, HALF)]
            dst = wd.at[pl.ds(HALF, HALF)]
        return pltpu.make_async_remote_copy(
            src_ref=src, dst_ref=dst, send_sem=w_s.at[k], recv_sem=w_r.at[k],
            device_id=partner, device_id_type=MESH,
        )

    for k in range(3):
        loads[3 + k].wait()
        weight_copy(k).start()

    row = lax.broadcasted_iota(jnp.int32, (128, 128), 0)
    lane = lax.broadcasted_iota(jnp.int32, (128, 128), 1)
    low = lane < ROWS
    same_chunk = ((row // 4) % 2 == 0) == low
    tri = jnp.where(row < lane, 1.0, 0.0).astype(BF16)
    expert = (16 * z + row // 8).astype(F32)
    rank = (row % 4).astype(F32)

    def disp(g, i):
        q = plane(i)
        return pltpu.make_async_remote_copy(
            src_ref=send.at[g, q], dst_ref=recv.at[g, p],
            send_sem=disp_s.at[g, q], recv_sem=disp_r.at[g, p],
            device_id=(z, q * 2 + core), device_id_type=MESH,
        )

    def disp_own(g):
        return pltpu.make_async_copy(send.at[g, p], recv.at[g, p], disp_r.at[g, p])

    def disp_recv(g, i):
        q = plane(i)
        return pltpu.make_async_remote_copy(
            src_ref=send.at[g, q], dst_ref=recv.at[g, q],
            send_sem=disp_s.at[g, q], recv_sem=disp_r.at[g, q],
            device_id=(z, q * 2 + core), device_id_type=MESH,
        )

    def dispatch(g):
        low8 = low[:8]
        ids = jnp.where(low8, meta[2 * g, 0:8, :], meta[2 * g + 1, 0:8, :])
        prob = jnp.where(low8, meta[2 * g, 8:16, :], meta[2 * g + 1, 8:16, :])
        hit = jnp.zeros((128, 128), F32)
        weight = jnp.zeros((128, 128), F32)
        for k in range(TOP):
            match = ids[k : k + 1, :] == expert
            hit = jnp.where(match, 1.0, hit)
            weight = jnp.where(match, prob[k : k + 1, :], weight)
        hit = jnp.where(same_chunk, hit, 0.0)
        before = jnp.dot(hit.astype(BF16), tri, preferred_element_type=F32)
        sel = jnp.where(before == rank, hit, 0.0)
        scale = jnp.sum(sel * weight, axis=1, keepdims=True)
        selt[g] = sel.T.astype(BF16)
        sel_rows = sel.astype(BF16)[:, : 2 * ROWS]

        def tile(j, carry):
            cols = pl.ds(pl.multiple_of(j * 512, 512), 512)
            t2 = tok[2 * g : 2 * g + 2, :, cols].reshape(2 * ROWS, 512)
            g2 = grad[2 * g : 2 * g + 2, :, cols].reshape(2 * ROWS, 512)
            a = jnp.dot(sel_rows, t2, preferred_element_type=F32)
            b = jnp.dot(sel_rows, g2, preferred_element_type=F32) * scale
            both = jnp.concatenate([a.reshape(16, 8, 512), b.reshape(16, 8, 512)], axis=1)
            send[g, :, :, cols] = both.astype(BF16)
            return carry

        lax.fori_loop(0, 4, tile, 0)

        def go(i, carry):
            disp(g, i).start()
            return carry

        lax.fori_loop(1, 16, go, 0)
        disp_own(g).start()

    def ret(g, i):
        q = plane(i)
        return pltpu.make_async_remote_copy(
            src_ref=rsend.at[g, q], dst_ref=rrecv.at[g, p],
            send_sem=ret_s.at[g, q], recv_sem=ret_r.at[g, p],
            device_id=(z, q * 2 + core), device_id_type=MESH,
        )

    def ret_own(g):
        return pltpu.make_async_copy(rsend.at[g, p], rrecv.at[g, p], ret_r.at[g, p])

    def ret_recv(g, i):
        q = plane(i)
        return pltpu.make_async_remote_copy(
            src_ref=rsend.at[g, q], dst_ref=rrecv.at[g, q],
            send_sem=ret_s.at[g, q], recv_sem=ret_r.at[g, q],
            device_id=(z, q * 2 + core), device_id_type=MESH,
        )

    def expert_rows(g):
        def landed(i, carry):
            disp_recv(g, i).wait_recv()
            return carry

        lax.fori_loop(1, 16, landed, 0)
        disp_own(g).wait()
        rows = pl.ds(g * 128, 128)

        def unpack(j, carry):
            cols = pl.ds(pl.multiple_of(j * 512, 512), 512)
            both = recv[g, :, :, cols].astype(F32)
            xs[rows, cols] = both[:, 0:8].reshape(128, 512).astype(BF16)
            gs[rows, cols] = both[:, 8:16].reshape(128, 512).astype(BF16)
            return carry

        lax.fori_loop(0, 4, unpack, 0)
        if g == 0:
            for k in range(3):
                weight_copy(k).wait_recv()

        def forward(h, carry):
            wide = pl.ds(pl.multiple_of(h * 2 * HALF, 2 * HALF), 2 * HALF)
            narrow = pl.ds(pl.multiple_of(h * HALF, HALF), HALF)
            pre = jnp.dot(xs[rows, :], wgu[:, wide], preferred_element_type=F32)
            gate, up = pre[:, :HALF], pre[:, HALF:]
            hidden_grad = lax.dot_general(gs[rows, :], wd[narrow, :], NT, preferred_element_type=F32)
            s = jax.nn.sigmoid(gate)
            act = gate * s
            hid[rows, narrow] = (act * up).astype(BF16)
            gate_in = (hidden_grad * up * s * (1.0 + gate * (1.0 - s))).astype(BF16)
            up_in = (hidden_grad * act).astype(BF16)
            giui[rows, wide] = jnp.concatenate([gate_in, up_in], axis=1)
            return carry

        lax.fori_loop(0, 2, forward, 0)

        def back(j, carry):
            out = pl.ds(pl.multiple_of(j * 512, 512), 512)
            right = pl.ds(pl.multiple_of(j * 512 + 1024, 512), 512)
            a = lax.dot_general(giui[rows, :], wgu[out, :], NT, preferred_element_type=F32)
            b = lax.dot_general(giui[rows, :], wgu[right, :], NT, preferred_element_type=F32)
            both = jnp.concatenate([a.reshape(16, 8, 512), b.reshape(16, 8, 512)], axis=1)
            rsend[g, :, :, out] = both.astype(BF16)
            return carry

        lax.fori_loop(0, 2, back, 0)

        def go(i, carry):
            ret(g, i).start()
            return carry

        lax.fori_loop(1, 16, go, 0)
        ret_own(g).start()

    def zcopy(j):
        return pltpu.make_async_remote_copy(
            src_ref=zsend.at[j], dst_ref=zrecv.at[j],
            send_sem=z_s.at[j], recv_sem=z_r.at[j],
            device_id=zdev(OFFSET[j]), device_id_type=MESH,
        )

    def combine(g):
        def landed(i, carry):
            ret_recv(g, i).wait_recv()
            return carry

        lax.fori_loop(1, 16, landed, 0)
        ret_own(g).wait()

        def tile(j, carry):
            both = rrecv[g, :, :, pl.ds(pl.multiple_of(j * 512, 512), 512)].astype(F32)
            for side in range(2):
                cols = pl.ds(pl.multiple_of(j * 512 + side * 1024, 512), 512)
                part = both[:, side * 8 : side * 8 + 8].reshape(128, 512).astype(BF16)
                total = jnp.dot(selt[g], part, preferred_element_type=F32)
                if g == 0:
                    own[:, cols] = total[:ROWS]
                else:
                    zsend[2 * g, :, cols] = total[:ROWS].astype(BF16)
                zsend[2 * g + 1, :, cols] = total[ROWS : 2 * ROWS].astype(BF16)
            return carry

        lax.fori_loop(0, 2, tile, 0)
        for j in (2 * g + 1, 2 * g):
            if j > 0:
                zcopy(j).start()

    def grad_copy(k):
        src, dst = ((gu_send.at[0], gu_recv.at[0]), (gu_send.at[1], gu_recv.at[1]), (d_send, d_recv))[k]
        return pltpu.make_async_remote_copy(
            src_ref=src, dst_ref=dst, send_sem=g_s.at[k], recv_sem=g_r.at[k],
            device_id=partner, device_id_type=MESH,
        )

    def gate_up_tile(j, h):
        rows = pl.ds(pl.multiple_of(j * 256, 256), 256)
        return rows, lax.dot_general(
            xs[:, rows], giui[:, h * 2 * HALF : (h + 1) * 2 * HALF], TN, preferred_element_type=F32
        )

    def down_tile(j, h):
        cols = pl.ds(pl.multiple_of(j * 512, 512), 512)
        return cols, lax.dot_general(
            hid[:, h * HALF : (h + 1) * HALF], gs[:, cols], TN, preferred_element_type=F32
        )

    def partner_grads():
        def tile(j, carry):
            rows, both = gate_up_tile(j, 1)
            gu_send[0, rows, :] = both[:, :HALF].astype(BF16)
            gu_send[1, rows, :] = both[:, HALF:].astype(BF16)
            return carry

        lax.fori_loop(0, 8, tile, 0)
        grad_copy(0).start()
        grad_copy(1).start()

        def tile_down(j, carry):
            cols, part = down_tile(j, 1)
            d_send[:, cols] = part.astype(BF16)
            return carry

        lax.fori_loop(0, 4, tile_down, 0)
        grad_copy(2).start()

    def own_grads():
        grad_copy(0).wait_recv()
        grad_copy(1).wait_recv()

        def tile(j, carry):
            rows, both = gate_up_tile(j, 0)
            gate_out[rows, :] = (both[:, :HALF] + gu_recv[0, rows, :].astype(F32)).astype(BF16)
            up_out[rows, :] = (both[:, HALF:] + gu_recv[1, rows, :].astype(F32)).astype(BF16)
            return carry

        lax.fori_loop(0, 8, tile, 0)
        grad_copy(2).wait_recv()

        def tile_down(j, carry):
            cols, part = down_tile(j, 0)
            down_out[:, cols] = (part + d_recv[:, cols].astype(F32)).astype(BF16)
            return carry

        lax.fori_loop(0, 4, tile_down, 0)

    advance(1)
    dispatch(0)
    advance(2)
    dispatch(1)
    expert_rows(0)
    advance(3)
    dispatch(2)
    expert_rows(1)
    advance(4)
    dispatch(3)
    combine(0)
    expert_rows(2)
    combine(1)
    expert_rows(3)
    partner_grads()
    combine(2)
    combine(3)
    own_grads()

    for j in range(1, REP):
        zcopy(j).wait_recv()

    def finish(j, carry):
        cols = pl.ds(pl.multiple_of(j * 512, 512), 512)
        total = own[:, cols]
        for k in range(1, REP):
            total = total + zrecv[k, :, cols].astype(F32)
        tok_out[:, cols] = total.astype(BF16)
        return carry

    lax.fori_loop(0, 4, finish, 0)

    for h in range(1, 5):
        for direction in (0, 1):
            for piece in pieces(direction, h):
                hop(direction, h, piece).wait_send()
    for k in range(3):
        weight_copy(k).wait_send()
        grad_copy(k).wait_send()
    for j in range(1, REP):
        zcopy(j).wait_send()

    def drain(i, carry):
        for g in range(GROUPS):
            disp(g, i).wait_send()
            ret(g, i).wait_send()
        return carry

    lax.fori_loop(1, 16, drain, 0)


def per_device(tokens, grad_out, expert_ids, gate_probs, gate_weight, up_weight, down_weight):
    def lay(values, fill):
        t = values.astype(F32).T
        pad = jnp.full((TOP, 128 - 2 * ROWS), fill, F32)
        return jnp.concatenate([t, t, pad], axis=1)

    meta = jnp.concatenate([lay(expert_ids, -1.0), lay(gate_probs, 0.0)], axis=0)
    anywhere = pl.BlockSpec(memory_space=pl.ANY)
    vmem = pl.BlockSpec(memory_space=pltpu.VMEM)
    dma = pltpu.SemaphoreType.DMA
    tok_grad, gate_grad, up_grad, down_grad = pl.pallas_call(
        kernel,
        out_shape=(
            jax.ShapeDtypeStruct((ROWS, D), BF16),
            jax.ShapeDtypeStruct((D, HALF), BF16),
            jax.ShapeDtypeStruct((D, HALF), BF16),
            jax.ShapeDtypeStruct((HALF, D), BF16),
        ),
        in_specs=[anywhere] * 6,
        out_specs=[vmem] * 4,
        scratch_shapes=[
            pltpu.VMEM((REP, ROWS, D), BF16),
            pltpu.VMEM((REP, ROWS, D), BF16),
            pltpu.VMEM((REP, 16, 128), F32),
            pltpu.VMEM((D, 4 * HALF), BF16),
            pltpu.VMEM((2 * HALF, D), BF16),
            pltpu.VMEM((GROUPS, 16, 16, D), BF16),
            pltpu.VMEM((GROUPS, 16, 16, D), BF16),
            pltpu.VMEM((GROUPS * 128, D), BF16),
            pltpu.VMEM((GROUPS * 128, D), BF16),
            pltpu.VMEM((GROUPS * 128, 2 * HALF), BF16),
            pltpu.VMEM((GROUPS * 128, 4 * HALF), BF16),
            pltpu.VMEM((GROUPS, 16, 16, D // 2), BF16),
            pltpu.VMEM((GROUPS, 16, 16, D // 2), BF16),
            pltpu.VMEM((GROUPS, 128, 128), BF16),
            pltpu.VMEM((REP, ROWS, D), BF16),
            pltpu.VMEM((REP, ROWS, D), BF16),
            pltpu.VMEM((ROWS, D), F32),
            pltpu.VMEM((2, D, HALF), BF16),
            pltpu.VMEM((2, D, HALF), BF16),
            pltpu.VMEM((HALF, D), BF16),
            pltpu.VMEM((HALF, D), BF16),
            dma((6,)),
            dma((2, 4, 3)),
            dma((2, 4, 3)),
            dma((3,)),
            dma((3,)),
            dma((GROUPS, 16)),
            dma((GROUPS, 16)),
            dma((GROUPS, 16)),
            dma((GROUPS, 16)),
            dma((REP,)),
            dma((REP,)),
            dma((3,)),
            dma((3,)),
        ],
        compiler_params=pltpu.CompilerParams(
            collective_id=0, has_side_effects=True, vmem_limit_bytes=60 * 2**20
        ),
    )(tokens, grad_out, meta, gate_weight[0], up_weight[0], down_weight[0])
    return tok_grad, gate_grad[None], up_grad[None], down_grad[None]


def solution(mesh):
    rows = P(("rep", "exp"), None)
    mats = P(("rep", "exp"), None, None)
    return jax.shard_map(
        per_device,
        mesh=mesh,
        in_specs=(rows, rows, rows, rows, mats, mats, mats),
        out_specs=(rows, mats, mats, mats),
        check_vma=False,
    )
```

```python
import jax
import jax.numpy as jnp
from jax import lax
from jax.experimental import pallas as pl
from jax.experimental.pallas import tpu as pltpu
from jax.sharding import PartitionSpec as P

MESH = pl.DeviceIdType.MESH
F32 = jnp.float32
BF16 = jnp.bfloat16
REP = 8
ROWS = 48
D = 2048
HALF = 384
TOP = 8
GROUPS = 4
LIMIT = 47
NT = (((1,), (1,)), ((), ()))
TN = (((0,), (0,)), ((), ()))


UP = (0, 1, 3, 5, 7)
DOWN = (0, 2, 4, 6, 7)
PAIRS = ((1, 2), (3, 4), (5, 6), (0, 7))


def kernel(
    tok_hbm, grad_hbm, ids_hbm, prob_hbm, gate_hbm, up_hbm, down_hbm,
    tok_out, gate_out, up_out, down_out,
    ids_in, prob_in, result, tok, grad, meta, wgu, wd, send, recv, ssend, srecv, xs, gs, hid, giui, rsend, rrecv, selt,
    zsend, zrecv, zhalf, own, gu_send, gu_recv, d_send, d_recv,
    load_sem, store_sem, ring_s, ring_r, w_s, w_r, disp_s, disp_r, ret_s, ret_r, z_s, z_r, g_s, g_r,
):
    z = lax.axis_index("rep")
    e = lax.axis_index("exp")
    p = e // 2
    core = e % 2
    px = p % 4
    py = p // 4
    partner = (z, p * 2 + 1 - core)

    def plane(i):
        return ((py + i // 4) % 4) * 4 + (px + i % 4) % 4

    def zdev(d):
        return ((z + d) % REP, e)

    loads = [
        pltpu.make_async_copy(ids_hbm, ids_in, load_sem.at[0]),
        pltpu.make_async_copy(prob_hbm, prob_in, load_sem.at[6]),
        pltpu.make_async_copy(tok_hbm, tok.at[0], load_sem.at[1]),
        pltpu.make_async_copy(grad_hbm, grad.at[0], load_sem.at[2]),
        pltpu.make_async_copy(gate_hbm, wgu.at[:, pl.ds(0, HALF)], load_sem.at[3]),
        pltpu.make_async_copy(up_hbm, wgu.at[:, pl.ds(HALF, HALF)], load_sem.at[4]),
        pltpu.make_async_copy(down_hbm, wd.at[pl.ds(0, HALF)], load_sem.at[5]),
    ]
    for c in loads:
        c.start()

    barrier = pltpu.get_barrier_semaphore()

    def greet_plane(i, carry):
        pl.semaphore_signal(barrier, inc=1, device_id=(z, plane(i) * 2 + core), device_id_type=MESH)
        return carry

    def greet_z(i, carry):
        pl.semaphore_signal(barrier, inc=1, device_id=zdev(i), device_id_type=MESH)
        return carry

    lax.fori_loop(1, 16, greet_plane, 0)
    lax.fori_loop(1, REP, greet_z, 0)
    pl.semaphore_signal(barrier, inc=1, device_id=partner, device_id_type=MESH)
    pl.semaphore_wait(barrier, 23)

    def hop(direction, h, piece):
        table = (UP, DOWN)[direction]
        buf = (tok, grad, meta)[piece]
        return pltpu.make_async_remote_copy(
            src_ref=buf.at[table[h - 1]],
            dst_ref=buf.at[table[h]],
            send_sem=ring_s.at[direction, h - 1, piece],
            recv_sem=ring_r.at[direction, h - 1, piece],
            device_id=zdev((1, 7)[direction]),
            device_id_type=MESH,
        )

    def pieces(direction, h):
        if h < 4:
            return (0, 1, 2)
        return ((0, 2), (1,))[direction]

    for c in loads[2:4]:
        c.wait()
    for piece in (0, 1):
        for direction in (0, 1):
            hop(direction, 1, piece).start()
    for c in loads[:2]:
        c.wait()

    def twice(values, fill):
        return jnp.concatenate([values, values, jnp.full((TOP, 128 - 2 * ROWS), fill, F32)], axis=1)

    meta[0, 0:8, :] = twice(ids_in[...].astype(F32), -1.0)
    meta[0, 8:16, :] = twice(prob_in[...], 0.0)
    for direction in (0, 1):
        hop(direction, 1, 2).start()

    def advance(h):
        for piece in (0, 1, 2):
            for direction in (0, 1):
                if piece in pieces(direction, h):
                    hop(direction, h, piece).wait_recv()
                    if h < 4 and piece in pieces(direction, h + 1):
                        hop(direction, h + 1, piece).start()

    def weight_copy(k):
        if k < 2:
            src = wgu.at[:, pl.ds(k * HALF, HALF)]
            dst = wgu.at[:, pl.ds((k + 2) * HALF, HALF)]
        else:
            src = wd.at[pl.ds(0, HALF)]
            dst = wd.at[pl.ds(HALF, HALF)]
        return pltpu.make_async_remote_copy(
            src_ref=src, dst_ref=dst, send_sem=w_s.at[k], recv_sem=w_r.at[k],
            device_id=partner, device_id_type=MESH,
        )

    row = lax.broadcasted_iota(jnp.int32, (128, 128), 0)
    lane = lax.broadcasted_iota(jnp.int32, (128, 128), 1)
    low = lane < ROWS
    same_chunk = ((row // 4) % 2 == 0) == low
    tri = jnp.where(row < lane, 1.0, 0.0).astype(BF16)
    expert = (16 * z + row // 8).astype(F32)
    rank = (row % 4).astype(F32)

    def disp_refs(g):
        if g < 3:
            return send.at[g], recv.at[g]
        return ssend.at[g - 3], srecv.at[g - 3]

    def disp(g, i):
        q = plane(i)
        src, dst = disp_refs(g)
        return pltpu.make_async_remote_copy(
            src_ref=src.at[q], dst_ref=dst.at[p],
            send_sem=disp_s.at[g, q], recv_sem=disp_r.at[g, p],
            device_id=(z, q * 2 + core), device_id_type=MESH,
        )

    def disp_own(g):
        src, dst = disp_refs(g)
        return pltpu.make_async_copy(src.at[p], dst.at[p], disp_r.at[g, p])

    def disp_recv(g, i):
        q = plane(i)
        src, dst = disp_refs(g)
        return pltpu.make_async_remote_copy(
            src_ref=src.at[q], dst_ref=dst.at[q],
            send_sem=disp_s.at[g, q], recv_sem=disp_r.at[g, q],
            device_id=(z, q * 2 + core), device_id_type=MESH,
        )

    def select(first, second):
        low8 = low[:8]
        ids = jnp.where(low8, meta[first, 0:8, :], meta[second, 0:8, :])
        prob = jnp.where(low8, meta[first, 8:16, :], meta[second, 8:16, :])
        hit = jnp.zeros((128, 128), F32)
        weight = jnp.zeros((128, 128), F32)
        for k in range(TOP):
            match = ids[k : k + 1, :] == expert
            hit = jnp.where(match, 1.0, hit)
            weight = jnp.where(match, prob[k : k + 1, :], weight)
        hit = jnp.where(same_chunk, hit, 0.0)
        before = jnp.dot(hit.astype(BF16), tri, preferred_element_type=F32)
        sel = jnp.where(before == rank, hit, 0.0)
        return sel, jnp.sum(sel * weight, axis=1, keepdims=True)

    def dispatch(g):
        single = g >= 3
        first, second = PAIRS[g] if not single else ((0, 0), (7, 7))[g - 3]
        sel, scale = select(first, second)
        if not single:
            selt[g] = sel.T.astype(BF16)
        sel_rows = sel.astype(BF16)[:, : 2 * ROWS]

        def tile(j, carry):
            cols = pl.ds(pl.multiple_of(j * 512, 512), 512)
            if single:
                right = pl.ds(pl.multiple_of(j * 512 + 1024, 512), 512)
                t2 = jnp.concatenate([tok[first, :, cols], tok[first, :, right]], axis=0)
                g2 = jnp.concatenate([grad[first, :, cols], grad[first, :, right]], axis=0)
            else:
                t2 = tok[first : first + 2, :, cols].reshape(2 * ROWS, 512)
                g2 = grad[first : first + 2, :, cols].reshape(2 * ROWS, 512)
            a = jnp.dot(sel_rows, t2, preferred_element_type=F32)
            b = jnp.dot(sel_rows, g2, preferred_element_type=F32) * scale
            both = jnp.concatenate([a.reshape(16, 8, 512), b.reshape(16, 8, 512)], axis=1)
            disp_refs(g)[0][:, :, cols] = both.astype(BF16)
            return carry

        lax.fori_loop(0, 2 if single else 4, tile, 0)

        def go(i, carry):
            disp(g, i).start()
            return carry

        lax.fori_loop(1, 16, go, 0)
        disp_own(g).start()

    def ret(g, i):
        q = plane(i)
        return pltpu.make_async_remote_copy(
            src_ref=rsend.at[g, q], dst_ref=rrecv.at[g, p],
            send_sem=ret_s.at[g, q], recv_sem=ret_r.at[g, p],
            device_id=(z, q * 2 + core), device_id_type=MESH,
        )

    def ret_own(g):
        return pltpu.make_async_copy(rsend.at[g, p], rrecv.at[g, p], ret_r.at[g, p])

    def ret_recv(g, i):
        q = plane(i)
        return pltpu.make_async_remote_copy(
            src_ref=rsend.at[g, q], dst_ref=rrecv.at[g, q],
            send_sem=ret_s.at[g, q], recv_sem=ret_r.at[g, q],
            device_id=(z, q * 2 + core), device_id_type=MESH,
        )

    def landed(g):
        def wait(i, carry):
            disp_recv(g, i).wait_recv()
            return carry

        lax.fori_loop(1, 16, wait, 0)
        disp_own(g).wait()

    def expert_rows(g):
        rows = pl.ds(g * 128, 128)
        landed(g)
        if g < 3:
            def unpack(j, carry):
                cols = pl.ds(pl.multiple_of(j * 512, 512), 512)
                both = recv[g, :, :, cols].astype(F32)
                xs[rows, cols] = both[:, 0:8].reshape(128, 512).astype(BF16)
                gs[rows, cols] = both[:, 8:16].reshape(128, 512).astype(BF16)
                return carry

            lax.fori_loop(0, 4, unpack, 0)
        else:
            landed(4)

            def unpack(j, carry):
                left = pl.multiple_of(j * 256, 256)
                near = srecv[0, :, :, pl.ds(left, 256)].astype(F32)
                far = srecv[1, :, :, pl.ds(left, 256)].astype(F32)
                for side in range(2):
                    cols = pl.ds(left + side * 1024, 256)
                    for out, base in ((xs, 0), (gs, 8)):
                        lo = base + 4 * side
                        both = jnp.concatenate([near[:, lo : lo + 4], far[:, lo : lo + 4]], axis=1)
                        out[rows, cols] = both.reshape(128, 256).astype(BF16)
                return carry

            lax.fori_loop(0, 4, unpack, 0)
        if g == 0:
            for k in range(3):
                weight_copy(k).wait_recv()

        def forward(h, carry):
            wide = pl.ds(pl.multiple_of(h * 2 * HALF, 2 * HALF), 2 * HALF)
            narrow = pl.ds(pl.multiple_of(h * HALF, HALF), HALF)
            pre = jnp.dot(xs[rows, :], wgu[:, wide], preferred_element_type=F32)
            gate, up = pre[:, :HALF], pre[:, HALF:]
            hidden_grad = lax.dot_general(gs[rows, :], wd[narrow, :], NT, preferred_element_type=F32)
            s = jax.nn.sigmoid(gate)
            act = gate * s
            hid[rows, narrow] = (act * up).astype(BF16)
            gate_in = (hidden_grad * up * s * (1.0 + gate * (1.0 - s))).astype(BF16)
            up_in = (hidden_grad * act).astype(BF16)
            giui[rows, wide] = jnp.concatenate([gate_in, up_in], axis=1)
            return carry

        lax.fori_loop(0, 2, forward, 0)

        def back(j, carry):
            out = pl.ds(pl.multiple_of(j * 512, 512), 512)
            right = pl.ds(pl.multiple_of(j * 512 + 1024, 512), 512)
            a = lax.dot_general(giui[rows, :], wgu[out, :], NT, preferred_element_type=F32)
            b = lax.dot_general(giui[rows, :], wgu[right, :], NT, preferred_element_type=F32)
            both = jnp.concatenate([a.reshape(16, 8, 512), b.reshape(16, 8, 512)], axis=1)
            rsend[g, :, :, out] = both.astype(BF16)
            return carry

        lax.fori_loop(0, 2, back, 0)

    def send_back(g):
        def go(i, carry):
            ret(g, i).start()
            return carry

        lax.fori_loop(1, 16, go, 0)
        ret_own(g).start()

    def ways(h, block):
        return (0, 1) if h < 4 else (block // 2,)

    def inward(direction, h, block):
        cols = pl.ds(block * 512, 512)
        if h == 4:
            dst = zhalf.at[:, cols]
        else:
            dst = zrecv.at[direction, h - 1, :, cols]
        return pltpu.make_async_remote_copy(
            src_ref=zsend.at[(UP, DOWN)[direction][h], :, cols], dst_ref=dst,
            send_sem=z_s.at[direction, h - 1, block], recv_sem=z_r.at[direction, h - 1, block],
            device_id=zdev((7, 1)[direction]), device_id_type=MESH,
        )

    def combine(g):
        first, second = PAIRS[g]

        def wait(i, carry):
            ret_recv(g, i).wait_recv()
            return carry

        lax.fori_loop(1, 16, wait, 0)
        ret_own(g).wait()
        for block in (0, 2, 1, 3):
            cols = pl.ds(block * 512, 512)
            narrow = pl.ds(block % 2 * 512, 512)
            side = block // 2
            part = rrecv[g, :, :, narrow].astype(F32)[:, side * 8 : side * 8 + 8]
            total = jnp.dot(selt[g], part.reshape(128, 512).astype(BF16), preferred_element_type=F32)
            near, far = total[:ROWS], total[ROWS : 2 * ROWS]
            if g < 3:
                for direction in ways(g + 2, block):
                    inward(direction, g + 2, block).wait_recv()
            if g < 2:
                near = near + zrecv[0, g + 1, :, cols].astype(F32)
                far = far + zrecv[1, g + 1, :, cols].astype(F32)
            elif g == 2 and side == 0:
                near = near + zhalf[:, cols].astype(F32)
            elif g == 2:
                far = far + zhalf[:, cols].astype(F32)
            if g < 3:
                zsend[first, :, cols] = near.astype(BF16)
            else:
                own[:, cols] = near
            zsend[second, :, cols] = far.astype(BF16)
            for direction in ways(g + 1, block):
                inward(direction, g + 1, block).start()

    def grad_copy(k):
        src, dst = ((gu_send.at[0], gu_recv.at[0]), (gu_send.at[1], gu_recv.at[1]), (d_send, d_recv))[k]
        return pltpu.make_async_remote_copy(
            src_ref=src, dst_ref=dst, send_sem=g_s.at[k], recv_sem=g_r.at[k],
            device_id=partner, device_id_type=MESH,
        )

    def gate_up_tile(j, h):
        rows = pl.ds(pl.multiple_of(j * 256, 256), 256)
        return rows, lax.dot_general(
            xs[:, rows], giui[:, h * 2 * HALF : (h + 1) * 2 * HALF], TN, preferred_element_type=F32
        )

    def down_tile(j, h):
        cols = pl.ds(pl.multiple_of(j * 512, 512), 512)
        return cols, lax.dot_general(
            hid[:, h * HALF : (h + 1) * HALF], gs[:, cols], TN, preferred_element_type=F32
        )

    def partner_grads():
        def tile(j, carry):
            rows, both = gate_up_tile(j, 1)
            gu_send[0, rows, :] = both[:, :HALF].astype(BF16)
            gu_send[1, rows, :] = both[:, HALF:].astype(BF16)
            return carry

        lax.fori_loop(0, 8, tile, 0)
        grad_copy(0).start()
        grad_copy(1).start()

        def tile_down(j, carry):
            cols, part = down_tile(j, 1)
            d_send[:, cols] = part.astype(BF16)
            return carry

        lax.fori_loop(0, 4, tile_down, 0)
        grad_copy(2).start()

    def store(k):
        src, dst = (
            (gu_recv.at[0], gate_out), (gu_recv.at[1], up_out), (d_recv, down_out), (result, tok_out)
        )[k]
        return pltpu.make_async_copy(src, dst, store_sem.at[k])

    def own_grads():
        grad_copy(0).wait_recv()
        grad_copy(1).wait_recv()

        def tile(j, carry):
            rows, both = gate_up_tile(j, 0)
            gu_recv[0, rows, :] = (both[:, :HALF] + gu_recv[0, rows, :].astype(F32)).astype(BF16)
            gu_recv[1, rows, :] = (both[:, HALF:] + gu_recv[1, rows, :].astype(F32)).astype(BF16)
            return carry

        lax.fori_loop(0, 8, tile, 0)
        store(0).start()
        store(1).start()
        grad_copy(2).wait_recv()

        def tile_down(j, carry):
            cols, part = down_tile(j, 0)
            d_recv[:, cols] = (part + d_recv[:, cols].astype(F32)).astype(BF16)
            return carry

        lax.fori_loop(0, 4, tile_down, 0)
        store(2).start()

    dispatch(3)
    for k in range(3):
        loads[4 + k].wait()
        weight_copy(k).start()
    advance(1)
    dispatch(0)
    advance(2)
    dispatch(1)
    advance(3)
    dispatch(2)
    advance(4)
    dispatch(4)
    selt[3] = select(*PAIRS[3])[0].T.astype(BF16)
    expert_rows(0)
    expert_rows(1)
    expert_rows(2)
    send_back(2)
    expert_rows(3)
    send_back(3)
    send_back(1)
    send_back(0)
    partner_grads()
    combine(3)
    combine(2)
    combine(1)
    combine(0)
    own_grads()
    for block in (0, 2, 1, 3):
        cols = pl.ds(block * 512, 512)
        for direction in (0, 1):
            inward(direction, 1, block).wait_recv()
        total = own[:, cols] + zrecv[0, 0, :, cols].astype(F32) + zrecv[1, 0, :, cols].astype(F32)
        result[:, cols] = total.astype(BF16)
    store(3).start()

    for h in range(1, 5):
        for direction in (0, 1):
            for piece in pieces(direction, h):
                hop(direction, h, piece).wait_send()
    for k in range(3):
        weight_copy(k).wait_send()
        grad_copy(k).wait_send()
    for h in range(1, 5):
        for block in range(4):
            for direction in ways(h, block):
                inward(direction, h, block).wait_send()

    def drain(i, carry):
        for g in range(GROUPS + 1):
            disp(g, i).wait_send()
        for g in range(GROUPS):
            ret(g, i).wait_send()
        return carry

    lax.fori_loop(1, 16, drain, 0)
    for k in range(4):
        store(k).wait()


def per_device(tokens, grad_out, expert_ids, gate_probs, gate_weight, up_weight, down_weight):
    anywhere = pl.BlockSpec(memory_space=pl.ANY)
    dma = pltpu.SemaphoreType.DMA
    tok_grad, gate_grad, up_grad, down_grad = pl.pallas_call(
        kernel,
        out_shape=(
            jax.ShapeDtypeStruct((ROWS, D), BF16),
            jax.ShapeDtypeStruct((D, HALF), BF16),
            jax.ShapeDtypeStruct((D, HALF), BF16),
            jax.ShapeDtypeStruct((HALF, D), BF16),
        ),
        in_specs=[pl.BlockSpec(memory_space=pltpu.HBM)] * 7,
        out_specs=[anywhere] * 4,
        scratch_shapes=[
            pltpu.VMEM((TOP, ROWS), jnp.int32),
            pltpu.VMEM((TOP, ROWS), F32),
            pltpu.VMEM((ROWS, D), BF16),
            pltpu.VMEM((REP, ROWS, D), BF16),
            pltpu.VMEM((REP, ROWS, D), BF16),
            pltpu.VMEM((REP, 16, 128), F32),
            pltpu.VMEM((D, 4 * HALF), BF16),
            pltpu.VMEM((2 * HALF, D), BF16),
            pltpu.VMEM((3, 16, 16, D), BF16),
            pltpu.VMEM((3, 16, 16, D), BF16),
            pltpu.VMEM((2, 16, 16, D // 2), BF16),
            pltpu.VMEM((2, 16, 16, D // 2), BF16),
            pltpu.VMEM((GROUPS * 128, D), BF16),
            pltpu.VMEM((GROUPS * 128, D), BF16),
            pltpu.VMEM((GROUPS * 128, 2 * HALF), BF16),
            pltpu.VMEM((GROUPS * 128, 4 * HALF), BF16),
            pltpu.VMEM((GROUPS, 16, 16, D // 2), BF16),
            pltpu.VMEM((GROUPS, 16, 16, D // 2), BF16),
            pltpu.VMEM((GROUPS, 128, 128), BF16),
            pltpu.VMEM((REP, ROWS, D), BF16),
            pltpu.VMEM((2, 3, ROWS, D), BF16),
            pltpu.VMEM((ROWS, D), BF16),
            pltpu.VMEM((ROWS, D), F32),
            pltpu.VMEM((2, D, HALF), BF16),
            pltpu.VMEM((2, D, HALF), BF16),
            pltpu.VMEM((HALF, D), BF16),
            pltpu.VMEM((HALF, D), BF16),
            dma((7,)),
            dma((4,)),
            dma((2, 4, 3)),
            dma((2, 4, 3)),
            dma((3,)),
            dma((3,)),
            dma((GROUPS + 1, 16)),
            dma((GROUPS + 1, 16)),
            dma((GROUPS, 16)),
            dma((GROUPS, 16)),
            dma((2, 4, 4)),
            dma((2, 4, 4)),
            dma((3,)),
            dma((3,)),
        ],
        compiler_params=pltpu.CompilerParams(
            collective_id=0, has_side_effects=True, vmem_limit_bytes=LIMIT * 2**20
        ),
    )(*(
        pltpu.with_memory_space_constraint(x, pltpu.HBM)
        for x in (
            tokens, grad_out, expert_ids.T, gate_probs.T, gate_weight[0], up_weight[0], down_weight[0]
        )
    ))
    return tok_grad, gate_grad[None], up_grad[None], down_grad[None]


def solution(mesh):
    rows = P(("rep", "exp"), None)
    mats = P(("rep", "exp"), None, None)
    return jax.shard_map(
        per_device,
        mesh=mesh,
        in_specs=(rows, rows, rows, rows, mats, mats, mats),
        out_specs=(rows, mats, mats, mats),
        check_vma=False,
    )
```

```python
import jax
import jax.numpy as jnp
from jax import lax
from jax.experimental import pallas as pl
from jax.experimental.pallas import tpu as pltpu
from jax.sharding import PartitionSpec as P

MESH = pl.DeviceIdType.MESH
F32 = jnp.float32
BF16 = jnp.bfloat16
REP = 8
ROWS = 48
D = 2048
HALF = 384
TOP = 8
GROUPS = 4
LIMIT = 47
NT = (((1,), (1,)), ((), ()))
TN = (((0,), (0,)), ((), ()))


UP = (0, 1, 3, 5, 7)
DOWN = (0, 2, 4, 6, 7)
PAIRS = ((1, 2), (3, 4), (5, 6), (0, 7))


def kernel(
    tok_hbm, grad_hbm, ids_hbm, prob_hbm, gate_hbm, up_hbm, down_hbm,
    tok_out, gate_out, up_out, down_out,
    ids_in, prob_in, result, tok, grad, meta, wgu, wd, send, recv, ssend, srecv, xs, gs, hid, giui, rsend, rrecv, srsend, srrecv, selt,
    zsend, zrecv, zhalf, own, gu_send, gu_recv, d_send, d_recv,
    load_sem, store_sem, ring_s, ring_r, w_s, w_r, disp_s, disp_r, ret_s, ret_r, z_s, z_r, g_s, g_r,
):
    z = lax.axis_index("rep")
    e = lax.axis_index("exp")
    p = e // 2
    core = e % 2
    px = p % 4
    py = p // 4
    partner = (z, p * 2 + 1 - core)

    def plane(i):
        return ((py + i // 4) % 4) * 4 + (px + i % 4) % 4

    def zdev(d):
        return ((z + d) % REP, e)

    loads = [
        pltpu.make_async_copy(ids_hbm, ids_in, load_sem.at[0]),
        pltpu.make_async_copy(prob_hbm, prob_in, load_sem.at[6]),
        pltpu.make_async_copy(tok_hbm, tok.at[0], load_sem.at[1]),
        pltpu.make_async_copy(grad_hbm, grad.at[0], load_sem.at[2]),
        pltpu.make_async_copy(gate_hbm, wgu.at[:, pl.ds(0, HALF)], load_sem.at[3]),
        pltpu.make_async_copy(up_hbm, wgu.at[:, pl.ds(HALF, HALF)], load_sem.at[4]),
        pltpu.make_async_copy(down_hbm, wd.at[pl.ds(0, HALF)], load_sem.at[5]),
    ]
    for c in loads:
        c.start()

    barrier = pltpu.get_barrier_semaphore()

    def greet_plane(i, carry):
        pl.semaphore_signal(barrier, inc=1, device_id=(z, plane(i) * 2 + core), device_id_type=MESH)
        return carry

    def greet_z(i, carry):
        pl.semaphore_signal(barrier, inc=1, device_id=zdev(i), device_id_type=MESH)
        return carry

    lax.fori_loop(1, 16, greet_plane, 0)
    lax.fori_loop(1, REP, greet_z, 0)
    pl.semaphore_signal(barrier, inc=1, device_id=partner, device_id_type=MESH)
    pl.semaphore_wait(barrier, 23)

    def hop(direction, h, piece):
        table = (UP, DOWN)[direction]
        buf = (tok, grad, meta)[piece]
        return pltpu.make_async_remote_copy(
            src_ref=buf.at[table[h - 1]],
            dst_ref=buf.at[table[h]],
            send_sem=ring_s.at[direction, h - 1, piece],
            recv_sem=ring_r.at[direction, h - 1, piece],
            device_id=zdev((1, 7)[direction]),
            device_id_type=MESH,
        )

    def pieces(direction, h):
        if h < 4:
            return (0, 1, 2)
        return ((0, 2), (1,))[direction]

    for c in loads[2:4]:
        c.wait()
    for direction in (0, 1):
        hop(direction, 1, 0).start()
    for c in loads[:2]:
        c.wait()

    def twice(values, fill):
        return jnp.concatenate([values, values, jnp.full((TOP, 128 - 2 * ROWS), fill, F32)], axis=1)

    meta[0, 0:8, :] = twice(ids_in[...].astype(F32), -1.0)
    meta[0, 8:16, :] = twice(prob_in[...], 0.0)
    for piece in (2, 1):
        for direction in (0, 1):
            hop(direction, 1, piece).start()

    def advance(h, chosen=(0, 2, 1)):
        for piece in chosen:
            for direction in (0, 1):
                if piece in pieces(direction, h):
                    hop(direction, h, piece).wait_recv()
                    if h < 4 and piece in pieces(direction, h + 1):
                        hop(direction, h + 1, piece).start()

    def weight_copy(k):
        if k < 2:
            src = wgu.at[:, pl.ds(k * HALF, HALF)]
            dst = wgu.at[:, pl.ds((k + 2) * HALF, HALF)]
        else:
            src = wd.at[pl.ds(0, HALF)]
            dst = wd.at[pl.ds(HALF, HALF)]
        return pltpu.make_async_remote_copy(
            src_ref=src, dst_ref=dst, send_sem=w_s.at[k], recv_sem=w_r.at[k],
            device_id=partner, device_id_type=MESH,
        )

    row = lax.broadcasted_iota(jnp.int32, (128, 128), 0)
    lane = lax.broadcasted_iota(jnp.int32, (128, 128), 1)
    low = lane < ROWS
    same_chunk = ((row // 4) % 2 == 0) == low
    tri = jnp.where(row < lane, 1.0, 0.0).astype(BF16)
    expert = (16 * z + row // 8).astype(F32)
    rank = (row % 4).astype(F32)

    def disp_refs(g):
        if g in (1, 2):
            return send.at[g - 1], recv.at[g - 1]
        slot = {3: 0, 4: 1, 0: 2, 5: 3}[g]
        return ssend.at[slot], srecv.at[slot]

    def disp(g, i):
        q = plane(i)
        src, dst = disp_refs(g)
        return pltpu.make_async_remote_copy(
            src_ref=src.at[q], dst_ref=dst.at[p],
            send_sem=disp_s.at[g, q], recv_sem=disp_r.at[g, p],
            device_id=(z, q * 2 + core), device_id_type=MESH,
        )

    def disp_own(g):
        src, dst = disp_refs(g)
        return pltpu.make_async_copy(src.at[p], dst.at[p], disp_r.at[g, p])

    def disp_recv(g, i):
        q = plane(i)
        src, dst = disp_refs(g)
        return pltpu.make_async_remote_copy(
            src_ref=src.at[q], dst_ref=dst.at[q],
            send_sem=disp_s.at[g, q], recv_sem=disp_r.at[g, q],
            device_id=(z, q * 2 + core), device_id_type=MESH,
        )

    def select(first, second):
        low8 = low[:8]
        ids = jnp.where(low8, meta[first, 0:8, :], meta[second, 0:8, :])
        prob = jnp.where(low8, meta[first, 8:16, :], meta[second, 8:16, :])
        hit = jnp.zeros((128, 128), F32)
        weight = jnp.zeros((128, 128), F32)
        for k in range(TOP):
            match = ids[k : k + 1, :] == expert
            hit = jnp.where(match, 1.0, hit)
            weight = jnp.where(match, prob[k : k + 1, :], weight)
        hit = jnp.where(same_chunk, hit, 0.0)
        before = jnp.dot(hit.astype(BF16), tri, preferred_element_type=F32)
        sel = jnp.where(before == rank, hit, 0.0)
        return sel, jnp.sum(sel * weight, axis=1, keepdims=True)

    def launch(g):
        def go(i, carry):
            disp(g, i).start()
            return carry

        lax.fori_loop(1, 16, go, 0)
        disp_own(g).start()

    def dispatch(g):
        single = g >= 3
        first, second = PAIRS[g] if not single else ((0, 0), (7, 7))[g - 3]
        sel, scale = select(first, second)
        if not single:
            selt[g] = sel.T.astype(BF16)
        sel_rows = sel.astype(BF16)[:, : 2 * ROWS]

        def tile(j, carry):
            cols = pl.ds(pl.multiple_of(j * 512, 512), 512)
            if single:
                right = pl.ds(pl.multiple_of(j * 512 + 1024, 512), 512)
                t2 = jnp.concatenate([tok[first, :, cols], tok[first, :, right]], axis=0)
                g2 = jnp.concatenate([grad[first, :, cols], grad[first, :, right]], axis=0)
            else:
                t2 = tok[first : first + 2, :, cols].reshape(2 * ROWS, 512)
                g2 = grad[first : first + 2, :, cols].reshape(2 * ROWS, 512)
            a = jnp.dot(sel_rows, t2, preferred_element_type=F32)
            b = jnp.dot(sel_rows, g2, preferred_element_type=F32) * scale
            both = jnp.concatenate([a.reshape(16, 8, 512), b.reshape(16, 8, 512)], axis=1)
            disp_refs(g)[0][:, :, cols] = both.astype(BF16)
            return carry

        lax.fori_loop(0, 2 if single else 4, tile, 0)
        launch(g)

    def dispatch_near(message, buf, sel_rows, scale):
        def tile(j, carry):
            cols = pl.ds(pl.multiple_of(j * 512, 512), 512)
            halves = []
            for side in range(2):
                from_cols = pl.ds(pl.multiple_of(j * 512 + side * 1024, 512), 512)
                rows2 = buf[1:3, :, from_cols].reshape(2 * ROWS, 512)
                part = jnp.dot(sel_rows, rows2, preferred_element_type=F32)
                if scale is not None:
                    part = part * scale
                halves.append(part.reshape(16, 8, 512))
            disp_refs(message)[0][:, :, cols] = jnp.concatenate(halves, axis=1).astype(BF16)
            return carry

        lax.fori_loop(0, 2, tile, 0)
        launch(message)

    def ret_refs(g):
        if g < 3:
            return rsend.at[g], rrecv.at[g]
        return srsend.at[g - 3], srrecv.at[g - 3]

    def ret(g, i):
        q = plane(i)
        src, dst = ret_refs(g)
        return pltpu.make_async_remote_copy(
            src_ref=src.at[q], dst_ref=dst.at[p],
            send_sem=ret_s.at[g, q], recv_sem=ret_r.at[g, p],
            device_id=(z, q * 2 + core), device_id_type=MESH,
        )

    def ret_own(g):
        src, dst = ret_refs(g)
        return pltpu.make_async_copy(src.at[p], dst.at[p], ret_r.at[g, p])

    def ret_recv(g, i):
        q = plane(i)
        src, dst = ret_refs(g)
        return pltpu.make_async_remote_copy(
            src_ref=src.at[q], dst_ref=dst.at[q],
            send_sem=ret_s.at[g, q], recv_sem=ret_r.at[g, q],
            device_id=(z, q * 2 + core), device_id_type=MESH,
        )

    def landed(g):
        def wait(i, carry):
            disp_recv(g, i).wait_recv()
            return carry

        lax.fori_loop(1, 16, wait, 0)
        disp_own(g).wait()

    def expert_rows(g):
        rows = pl.ds(g * 128, 128)
        landed(g)
        if g == 0:
            landed(5)

            def unpack(j, carry):
                left = pl.multiple_of(j * 512, 512)
                for slot, out in ((2, xs), (3, gs)):
                    both = srecv[slot, :, :, pl.ds(left, 512)].astype(F32)
                    out[rows, pl.ds(left, 512)] = both[:, 0:8].reshape(128, 512).astype(BF16)
                    out[rows, pl.ds(left + 1024, 512)] = both[:, 8:16].reshape(128, 512).astype(BF16)
                return carry

            lax.fori_loop(0, 2, unpack, 0)
        elif g < 3:
            def unpack(j, carry):
                cols = pl.ds(pl.multiple_of(j * 512, 512), 512)
                both = recv[g - 1, :, :, cols].astype(F32)
                xs[rows, cols] = both[:, 0:8].reshape(128, 512).astype(BF16)
                gs[rows, cols] = both[:, 8:16].reshape(128, 512).astype(BF16)
                return carry

            lax.fori_loop(0, 4, unpack, 0)
        else:
            landed(4)

            def unpack(j, carry):
                left = pl.multiple_of(j * 256, 256)
                near = srecv[0, :, :, pl.ds(left, 256)].astype(F32)
                far = srecv[1, :, :, pl.ds(left, 256)].astype(F32)
                for side in range(2):
                    cols = pl.ds(left + side * 1024, 256)
                    for out, base in ((xs, 0), (gs, 8)):
                        lo = base + 4 * side
                        both = jnp.concatenate([near[:, lo : lo + 4], far[:, lo : lo + 4]], axis=1)
                        out[rows, cols] = both.reshape(128, 256).astype(BF16)
                return carry

            lax.fori_loop(0, 4, unpack, 0)
        if g == 0:
            for k in range(3):
                weight_copy(k).wait_recv()

        def forward(h, carry):
            wide = pl.ds(pl.multiple_of(h * 2 * HALF, 2 * HALF), 2 * HALF)
            narrow = pl.ds(pl.multiple_of(h * HALF, HALF), HALF)
            pre = jnp.dot(xs[rows, :], wgu[:, wide], preferred_element_type=F32)
            gate, up = pre[:, :HALF], pre[:, HALF:]
            hidden_grad = lax.dot_general(gs[rows, :], wd[narrow, :], NT, preferred_element_type=F32)
            s = jax.nn.sigmoid(gate)
            act = gate * s
            hid[rows, narrow] = (act * up).astype(BF16)
            gate_in = (hidden_grad * up * s * (1.0 + gate * (1.0 - s))).astype(BF16)
            up_in = (hidden_grad * act).astype(BF16)
            giui[rows, wide] = jnp.concatenate([gate_in, up_in], axis=1)
            return carry

        lax.fori_loop(0, 2, forward, 0)

        if g == 3:
            def back_single(j, carry):
                cols = pl.ds(pl.multiple_of(j * 256, 256), 256)
                parts = []
                for q in range(4):
                    feats = pl.ds(pl.multiple_of(j * 256 + q * 512, 256), 256)
                    a = lax.dot_general(giui[rows, :], wgu[feats, :], NT, preferred_element_type=F32)
                    parts.append(a.reshape(16, 8, 256))
                for c in range(2):
                    packed = jnp.concatenate([a[:, c * 4 : c * 4 + 4] for a in parts], axis=1)
                    srsend[c, :, :, cols] = packed.astype(BF16)
                return carry

            lax.fori_loop(0, 2, back_single, 0)
            return

        def back(j, carry):
            out = pl.ds(pl.multiple_of(j * 512, 512), 512)
            right = pl.ds(pl.multiple_of(j * 512 + 1024, 512), 512)
            a = lax.dot_general(giui[rows, :], wgu[out, :], NT, preferred_element_type=F32)
            b = lax.dot_general(giui[rows, :], wgu[right, :], NT, preferred_element_type=F32)
            both = jnp.concatenate([a.reshape(16, 8, 512), b.reshape(16, 8, 512)], axis=1)
            rsend[g, :, :, out] = both.astype(BF16)
            return carry

        lax.fori_loop(0, 2, back, 0)

    def send_back(g):
        def go(i, carry):
            ret(g, i).start()
            return carry

        lax.fori_loop(1, 16, go, 0)
        ret_own(g).start()

    def ways(h, block):
        return (0, 1) if h < 4 else (block // 2,)

    def inward(direction, h, block):
        cols = pl.ds(block * 512, 512)
        if h == 4:
            dst = zhalf.at[:, cols]
        else:
            dst = zrecv.at[direction, h - 1, :, cols]
        return pltpu.make_async_remote_copy(
            src_ref=zsend.at[(UP, DOWN)[direction][h], :, cols], dst_ref=dst,
            send_sem=z_s.at[direction, h - 1, block], recv_sem=z_r.at[direction, h - 1, block],
            device_id=zdev((7, 1)[direction]), device_id_type=MESH,
        )

    def returned(g):
        def wait(i, carry):
            ret_recv(g, i).wait_recv()
            return carry

        lax.fori_loop(1, 16, wait, 0)
        ret_own(g).wait()

    def combine_single(c):
        returned(3 + c)
        for block in (0, 2, 1, 3):
            cols = pl.ds(block * 512, 512)
            part = srrecv[c, :, :, :].astype(F32)[:, block * 4 : block * 4 + 4]
            part = jnp.concatenate([part, part], axis=1).reshape(128, 512).astype(BF16)
            total = jnp.dot(selt[3], part, preferred_element_type=F32)
            if c == 0:
                own[:, cols] = total[:ROWS]
            else:
                zsend[7, :, cols] = total[ROWS : 2 * ROWS].astype(BF16)
                for direction in ways(4, block):
                    inward(direction, 4, block).start()

    def combine(g):
        first, second = PAIRS[g]
        returned(g)
        for block in (0, 2, 1, 3):
            cols = pl.ds(block * 512, 512)
            narrow = pl.ds(block % 2 * 512, 512)
            side = block // 2
            part = rrecv[g, :, :, narrow].astype(F32)[:, side * 8 : side * 8 + 8]
            total = jnp.dot(selt[g], part.reshape(128, 512).astype(BF16), preferred_element_type=F32)
            near, far = total[:ROWS], total[ROWS : 2 * ROWS]
            for direction in ways(g + 2, block):
                inward(direction, g + 2, block).wait_recv()
            if g < 2:
                near = near + zrecv[0, g + 1, :, cols].astype(F32)
                far = far + zrecv[1, g + 1, :, cols].astype(F32)
            elif side == 0:
                near = near + zhalf[:, cols].astype(F32)
            else:
                far = far + zhalf[:, cols].astype(F32)
            zsend[first, :, cols] = near.astype(BF16)
            zsend[second, :, cols] = far.astype(BF16)
            for direction in (0, 1):
                inward(direction, g + 1, block).start()

    def grad_copy(k):
        src, dst = ((gu_send.at[0], gu_recv.at[0]), (gu_send.at[1], gu_recv.at[1]), (d_send, d_recv))[k]
        return pltpu.make_async_remote_copy(
            src_ref=src, dst_ref=dst, send_sem=g_s.at[k], recv_sem=g_r.at[k],
            device_id=partner, device_id_type=MESH,
        )

    def gate_up_tile(j, h):
        rows = pl.ds(pl.multiple_of(j * 256, 256), 256)
        return rows, lax.dot_general(
            xs[:, rows], giui[:, h * 2 * HALF : (h + 1) * 2 * HALF], TN, preferred_element_type=F32
        )

    def down_tile(j, h):
        cols = pl.ds(pl.multiple_of(j * 512, 512), 512)
        return cols, lax.dot_general(
            hid[:, h * HALF : (h + 1) * HALF], gs[:, cols], TN, preferred_element_type=F32
        )

    def partner_grads():
        def tile(j, carry):
            rows, both = gate_up_tile(j, 1)
            gu_send[0, rows, :] = both[:, :HALF].astype(BF16)
            gu_send[1, rows, :] = both[:, HALF:].astype(BF16)
            return carry

        lax.fori_loop(0, 8, tile, 0)
        grad_copy(0).start()
        grad_copy(1).start()

        def tile_down(j, carry):
            cols, part = down_tile(j, 1)
            d_send[:, cols] = part.astype(BF16)
            return carry

        lax.fori_loop(0, 4, tile_down, 0)
        grad_copy(2).start()

    def store(k):
        src, dst = (
            (gu_recv.at[0], gate_out), (gu_recv.at[1], up_out), (d_recv, down_out), (result, tok_out)
        )[k]
        return pltpu.make_async_copy(src, dst, store_sem.at[k])

    def own_grads():
        grad_copy(0).wait_recv()
        grad_copy(1).wait_recv()

        def tile(j, carry):
            rows, both = gate_up_tile(j, 0)
            gu_recv[0, rows, :] = (both[:, :HALF] + gu_recv[0, rows, :].astype(F32)).astype(BF16)
            gu_recv[1, rows, :] = (both[:, HALF:] + gu_recv[1, rows, :].astype(F32)).astype(BF16)
            return carry

        lax.fori_loop(0, 8, tile, 0)
        store(0).start()
        store(1).start()
        grad_copy(2).wait_recv()

        def tile_down(j, carry):
            cols, part = down_tile(j, 0)
            d_recv[:, cols] = (part + d_recv[:, cols].astype(F32)).astype(BF16)
            return carry

        lax.fori_loop(0, 4, tile_down, 0)
        store(2).start()

    dispatch(3)
    for k in range(3):
        loads[4 + k].wait()
        weight_copy(k).start()
    advance(1, (0, 2))
    near_sel, near_scale = select(1, 2)
    selt[0] = near_sel.T.astype(BF16)
    near_rows = near_sel.astype(BF16)[:, : 2 * ROWS]
    dispatch_near(0, tok, near_rows, None)
    advance(1, (1,))
    dispatch_near(5, grad, near_rows, near_scale)
    advance(2)
    dispatch(1)
    advance(3)
    dispatch(2)
    advance(4)
    dispatch(4)
    selt[3] = select(*PAIRS[3])[0].T.astype(BF16)
    expert_rows(0)
    expert_rows(1)
    expert_rows(2)
    send_back(2)
    expert_rows(3)
    send_back(4)
    send_back(1)
    send_back(0)
    send_back(3)
    partner_grads()
    combine_single(1)
    combine(2)
    combine(1)
    combine(0)
    own_grads()
    combine_single(0)
    for block in (0, 2, 1, 3):
        cols = pl.ds(block * 512, 512)
        for direction in (0, 1):
            inward(direction, 1, block).wait_recv()
        total = own[:, cols] + zrecv[0, 0, :, cols].astype(F32) + zrecv[1, 0, :, cols].astype(F32)
        result[:, cols] = total.astype(BF16)
    store(3).start()

    for h in range(1, 5):
        for direction in (0, 1):
            for piece in pieces(direction, h):
                hop(direction, h, piece).wait_send()
    for k in range(3):
        weight_copy(k).wait_send()
        grad_copy(k).wait_send()
    for h in range(1, 5):
        for block in range(4):
            for direction in ways(h, block):
                inward(direction, h, block).wait_send()

    def drain(i, carry):
        for g in range(6):
            disp(g, i).wait_send()
        for g in range(5):
            ret(g, i).wait_send()
        return carry

    lax.fori_loop(1, 16, drain, 0)
    for k in range(4):
        store(k).wait()


def store_out(*refs):
    sems = refs[8]
    copies = [pltpu.make_async_copy(refs[k], refs[4 + k], sems.at[k]) for k in range(4)]
    for c in copies:
        c.start()
    for c in copies:
        c.wait()


def per_device(tokens, grad_out, expert_ids, gate_probs, gate_weight, up_weight, down_weight):
    anywhere = pl.BlockSpec(memory_space=pl.ANY)
    dma = pltpu.SemaphoreType.DMA
    tok_grad, gate_grad, up_grad, down_grad = pl.pallas_call(
        kernel,
        out_shape=(
            jax.ShapeDtypeStruct((ROWS, D), BF16),
            jax.ShapeDtypeStruct((D, HALF), BF16),
            jax.ShapeDtypeStruct((D, HALF), BF16),
            jax.ShapeDtypeStruct((HALF, D), BF16),
        ),
        in_specs=[pl.BlockSpec(memory_space=pltpu.HBM)] * 7,
        out_specs=[anywhere] * 4,
        scratch_shapes=[
            pltpu.VMEM((TOP, ROWS), jnp.int32),
            pltpu.VMEM((TOP, ROWS), F32),
            pltpu.VMEM((ROWS, D), BF16),
            pltpu.VMEM((REP, ROWS, D), BF16),
            pltpu.VMEM((REP, ROWS, D), BF16),
            pltpu.VMEM((REP, 16, 128), F32),
            pltpu.VMEM((D, 4 * HALF), BF16),
            pltpu.VMEM((2 * HALF, D), BF16),
            pltpu.VMEM((2, 16, 16, D), BF16),
            pltpu.VMEM((2, 16, 16, D), BF16),
            pltpu.VMEM((4, 16, 16, D // 2), BF16),
            pltpu.VMEM((4, 16, 16, D // 2), BF16),
            pltpu.VMEM((GROUPS * 128, D), BF16),
            pltpu.VMEM((GROUPS * 128, D), BF16),
            pltpu.VMEM((GROUPS * 128, 2 * HALF), BF16),
            pltpu.VMEM((GROUPS * 128, 4 * HALF), BF16),
            pltpu.VMEM((3, 16, 16, D // 2), BF16),
            pltpu.VMEM((3, 16, 16, D // 2), BF16),
            pltpu.VMEM((2, 16, 16, D // 4), BF16),
            pltpu.VMEM((2, 16, 16, D // 4), BF16),
            pltpu.VMEM((GROUPS, 128, 128), BF16),
            pltpu.VMEM((REP, ROWS, D), BF16),
            pltpu.VMEM((2, 3, ROWS, D), BF16),
            pltpu.VMEM((ROWS, D), BF16),
            pltpu.VMEM((ROWS, D), F32),
            pltpu.VMEM((2, D, HALF), BF16),
            pltpu.VMEM((2, D, HALF), BF16),
            pltpu.VMEM((HALF, D), BF16),
            pltpu.VMEM((HALF, D), BF16),
            dma((7,)),
            dma((4,)),
            dma((2, 4, 3)),
            dma((2, 4, 3)),
            dma((3,)),
            dma((3,)),
            dma((6, 16)),
            dma((6, 16)),
            dma((5, 16)),
            dma((5, 16)),
            dma((2, 4, 4)),
            dma((2, 4, 4)),
            dma((3,)),
            dma((3,)),
        ],
        compiler_params=pltpu.CompilerParams(
            collective_id=0, has_side_effects=True, vmem_limit_bytes=LIMIT * 2**20
        ),
    )(*(
        pltpu.with_memory_space_constraint(x, pltpu.HBM)
        for x in (
            tokens, grad_out, expert_ids.T, gate_probs.T, gate_weight[0], up_weight[0], down_weight[0]
        )
    ))
    outs = (tok_grad, gate_grad, up_grad, down_grad)
    tok_grad, gate_grad, up_grad, down_grad = pl.pallas_call(
        store_out,
        out_shape=tuple(jax.ShapeDtypeStruct(x.shape, x.dtype) for x in outs),
        in_specs=[anywhere] * 4,
        out_specs=[anywhere] * 4,
        scratch_shapes=[dma((4,))],
        compiler_params=pltpu.CompilerParams(vmem_limit_bytes=2**20),
    )(*outs)
    return tok_grad, gate_grad[None], up_grad[None], down_grad[None]


def solution(mesh):
    rows = P(("rep", "exp"), None)
    mats = P(("rep", "exp"), None, None)
    return jax.shard_map(
        per_device,
        mesh=mesh,
        in_specs=(rows, rows, rows, rows, mats, mats, mats),
        out_specs=(rows, mats, mats, mats),
        check_vma=False,
    )
```

```python
import jax
import jax.numpy as jnp
from jax import lax
from jax.experimental import pallas as pl
from jax.experimental.pallas import tpu as pltpu
from jax.sharding import PartitionSpec as P

MESH = pl.DeviceIdType.MESH
F32 = jnp.float32
BF16 = jnp.bfloat16
REP = 8
ROWS = 48
D = 2048
HALF = 384
TOP = 8
GROUPS = 4
LIMIT = 44
NT = (((1,), (1,)), ((), ()))
TN = (((0,), (0,)), ((), ()))


UP = (0, 1, 3, 5, 7)
DOWN = (0, 2, 4, 6, 7)
PAIRS = ((1, 2), (3, 4), (5, 6), (0, 7))


def kernel(
    tok_hbm, grad_hbm, ids_hbm, prob_hbm, gate_hbm, up_hbm, down_hbm,
    tok_out, gate_out, up_out, down_out,
    ids_in, prob_in, result, tok, grad, meta, wgu, wd, send, recv, ssend, srecv, xs, gs, hid, giui, rsend, rrecv, srsend, srrecv, selt,
    zsend, zrecv, zhalf, own, gu_recv, d_recv,
    load_sem, store_sem, ring_s, ring_r, w_s, w_r, disp_s, disp_r, ret_s, ret_r, z_s, z_r, g_s, g_r,
):
    z = lax.axis_index("rep")
    e = lax.axis_index("exp")
    p = e // 2
    core = e % 2
    px = p % 4
    py = p // 4
    partner = (z, p * 2 + 1 - core)

    def plane(i):
        return ((py + i // 4) % 4) * 4 + (px + i % 4) % 4

    def zdev(d):
        return ((z + d) % REP, e)

    loads = [
        pltpu.make_async_copy(ids_hbm, ids_in, load_sem.at[0]),
        pltpu.make_async_copy(prob_hbm, prob_in, load_sem.at[6]),
        pltpu.make_async_copy(tok_hbm, tok.at[0], load_sem.at[1]),
        pltpu.make_async_copy(grad_hbm, grad.at[0], load_sem.at[2]),
        pltpu.make_async_copy(gate_hbm, wgu.at[:, pl.ds(0, HALF)], load_sem.at[3]),
        pltpu.make_async_copy(up_hbm, wgu.at[:, pl.ds(HALF, HALF)], load_sem.at[4]),
        pltpu.make_async_copy(down_hbm, wd.at[pl.ds(0, HALF)], load_sem.at[5]),
    ]
    for c in loads:
        c.start()

    barrier = pltpu.get_barrier_semaphore()

    def greet_plane(i, carry):
        pl.semaphore_signal(barrier, inc=1, device_id=(z, plane(i) * 2 + core), device_id_type=MESH)
        return carry

    def greet_z(i, carry):
        pl.semaphore_signal(barrier, inc=1, device_id=zdev(i), device_id_type=MESH)
        return carry

    lax.fori_loop(1, 16, greet_plane, 0)
    lax.fori_loop(1, REP, greet_z, 0)
    pl.semaphore_signal(barrier, inc=1, device_id=partner, device_id_type=MESH)
    pl.semaphore_wait(barrier, 23)

    def hop(direction, h, piece):
        table = (UP, DOWN)[direction]
        buf = (tok, grad, meta)[piece]
        return pltpu.make_async_remote_copy(
            src_ref=buf.at[table[h - 1]],
            dst_ref=buf.at[table[h]],
            send_sem=ring_s.at[direction, h - 1, piece],
            recv_sem=ring_r.at[direction, h - 1, piece],
            device_id=zdev((1, 7)[direction]),
            device_id_type=MESH,
        )

    def pieces(direction, h):
        if h < 4:
            return (0, 1, 2)
        return ((0, 2), (1,))[direction]

    for c in loads[2:4]:
        c.wait()
    for direction in (0, 1):
        hop(direction, 1, 0).start()
    for c in loads[:2]:
        c.wait()

    def twice(values, fill):
        return jnp.concatenate([values, values, jnp.full((TOP, 128 - 2 * ROWS), fill, F32)], axis=1)

    meta[0, 0:8, :] = twice(ids_in[...].astype(F32), -1.0)
    meta[0, 8:16, :] = twice(prob_in[...], 0.0)
    for piece in (2, 1):
        for direction in (0, 1):
            hop(direction, 1, piece).start()

    def advance(h, chosen=(0, 2, 1)):
        for piece in chosen:
            for direction in (0, 1):
                if piece in pieces(direction, h):
                    hop(direction, h, piece).wait_recv()
                    if h < 4 and piece in pieces(direction, h + 1):
                        hop(direction, h + 1, piece).start()

    def weight_copy(k):
        if k < 2:
            src = wgu.at[:, pl.ds(k * HALF, HALF)]
            dst = wgu.at[:, pl.ds((k + 2) * HALF, HALF)]
        else:
            src = wd.at[pl.ds(0, HALF)]
            dst = wd.at[pl.ds(HALF, HALF)]
        return pltpu.make_async_remote_copy(
            src_ref=src, dst_ref=dst, send_sem=w_s.at[k], recv_sem=w_r.at[k],
            device_id=partner, device_id_type=MESH,
        )

    row = lax.broadcasted_iota(jnp.int32, (128, 128), 0)
    lane = lax.broadcasted_iota(jnp.int32, (128, 128), 1)
    low = lane < ROWS
    same_chunk = ((row // 4) % 2 == 0) == low
    tri = jnp.where(row < lane, 1.0, 0.0).astype(BF16)
    expert = (16 * z + row // 8).astype(F32)
    rank = (row % 4).astype(F32)

    def disp_refs(g):
        if g in (1, 2):
            return send.at[g - 1], recv.at[g - 1]
        slot = {3: 0, 4: 1, 0: 2, 5: 3}[g]
        return ssend.at[slot], srecv.at[slot]

    def disp(g, i):
        q = plane(i)
        src, dst = disp_refs(g)
        return pltpu.make_async_remote_copy(
            src_ref=src.at[q], dst_ref=dst.at[p],
            send_sem=disp_s.at[g, q], recv_sem=disp_r.at[g, p],
            device_id=(z, q * 2 + core), device_id_type=MESH,
        )

    def disp_own(g):
        src, dst = disp_refs(g)
        return pltpu.make_async_copy(src.at[p], dst.at[p], disp_r.at[g, p])

    def disp_recv(g, i):
        q = plane(i)
        src, dst = disp_refs(g)
        return pltpu.make_async_remote_copy(
            src_ref=src.at[q], dst_ref=dst.at[q],
            send_sem=disp_s.at[g, q], recv_sem=disp_r.at[g, q],
            device_id=(z, q * 2 + core), device_id_type=MESH,
        )

    def select(first, second):
        low8 = low[:8]
        ids = jnp.where(low8, meta[first, 0:8, :], meta[second, 0:8, :])
        prob = jnp.where(low8, meta[first, 8:16, :], meta[second, 8:16, :])
        hit = jnp.zeros((128, 128), F32)
        weight = jnp.zeros((128, 128), F32)
        for k in range(TOP):
            match = ids[k : k + 1, :] == expert
            hit = jnp.where(match, 1.0, hit)
            weight = jnp.where(match, prob[k : k + 1, :], weight)
        hit = jnp.where(same_chunk, hit, 0.0)
        before = jnp.dot(hit.astype(BF16), tri, preferred_element_type=F32)
        sel = jnp.where(before == rank, hit, 0.0)
        return sel, jnp.sum(sel * weight, axis=1, keepdims=True)

    def launch(g):
        def go(i, carry):
            disp(g, i).start()
            return carry

        lax.fori_loop(1, 16, go, 0)
        disp_own(g).start()

    def dispatch(g):
        single = g >= 3
        first, second = PAIRS[g] if not single else ((0, 0), (7, 7))[g - 3]
        sel, scale = select(first, second)
        if not single:
            selt[g] = sel.T.astype(BF16)
        sel_rows = sel.astype(BF16)[:, : 2 * ROWS]

        def tile(j, carry):
            cols = pl.ds(pl.multiple_of(j * 512, 512), 512)
            if single:
                right = pl.ds(pl.multiple_of(j * 512 + 1024, 512), 512)
                t2 = jnp.concatenate([tok[first, :, cols], tok[first, :, right]], axis=0)
                g2 = jnp.concatenate([grad[first, :, cols], grad[first, :, right]], axis=0)
            else:
                t2 = tok[first : first + 2, :, cols].reshape(2 * ROWS, 512)
                g2 = grad[first : first + 2, :, cols].reshape(2 * ROWS, 512)
            a = jnp.dot(sel_rows, t2, preferred_element_type=F32)
            b = jnp.dot(sel_rows, g2, preferred_element_type=F32) * scale
            both = jnp.concatenate([a.reshape(16, 8, 512), b.reshape(16, 8, 512)], axis=1)
            disp_refs(g)[0][:, :, cols] = both.astype(BF16)
            return carry

        lax.fori_loop(0, 2 if single else 4, tile, 0)
        launch(g)

    def dispatch_near(message, buf, sel_rows, scale):
        def tile(j, carry):
            cols = pl.ds(pl.multiple_of(j * 512, 512), 512)
            halves = []
            for side in range(2):
                from_cols = pl.ds(pl.multiple_of(j * 512 + side * 1024, 512), 512)
                rows2 = buf[1:3, :, from_cols].reshape(2 * ROWS, 512)
                part = jnp.dot(sel_rows, rows2, preferred_element_type=F32)
                if scale is not None:
                    part = part * scale
                halves.append(part.reshape(16, 8, 512))
            disp_refs(message)[0][:, :, cols] = jnp.concatenate(halves, axis=1).astype(BF16)
            return carry

        lax.fori_loop(0, 2, tile, 0)
        launch(message)

    def ret_refs(g):
        if g < 3:
            return rsend.at[g], rrecv.at[g]
        return srsend.at[g - 3], srrecv.at[g - 3]

    def ret(g, i):
        q = plane(i)
        src, dst = ret_refs(g)
        return pltpu.make_async_remote_copy(
            src_ref=src.at[q], dst_ref=dst.at[p],
            send_sem=ret_s.at[g, q], recv_sem=ret_r.at[g, p],
            device_id=(z, q * 2 + core), device_id_type=MESH,
        )

    def ret_own(g):
        src, dst = ret_refs(g)
        return pltpu.make_async_copy(src.at[p], dst.at[p], ret_r.at[g, p])

    def ret_recv(g, i):
        q = plane(i)
        src, dst = ret_refs(g)
        return pltpu.make_async_remote_copy(
            src_ref=src.at[q], dst_ref=dst.at[q],
            send_sem=ret_s.at[g, q], recv_sem=ret_r.at[g, q],
            device_id=(z, q * 2 + core), device_id_type=MESH,
        )

    def landed(g):
        def wait(i, carry):
            disp_recv(g, i).wait_recv()
            return carry

        lax.fori_loop(1, 16, wait, 0)
        disp_own(g).wait()

    def expert_rows(g):
        rows = pl.ds(g * 128, 128)
        landed(g)
        if g == 0:
            landed(5)

            def unpack(j, carry):
                left = pl.multiple_of(j * 512, 512)
                for slot, out in ((2, xs), (3, gs)):
                    both = srecv[slot, :, :, pl.ds(left, 512)].astype(F32)
                    out[rows, pl.ds(left, 512)] = both[:, 0:8].reshape(128, 512).astype(BF16)
                    out[rows, pl.ds(left + 1024, 512)] = both[:, 8:16].reshape(128, 512).astype(BF16)
                return carry

            lax.fori_loop(0, 2, unpack, 0)
        elif g < 3:
            def unpack(j, carry):
                cols = pl.ds(pl.multiple_of(j * 512, 512), 512)
                both = recv[g - 1, :, :, cols].astype(F32)
                xs[rows, cols] = both[:, 0:8].reshape(128, 512).astype(BF16)
                gs[rows, cols] = both[:, 8:16].reshape(128, 512).astype(BF16)
                return carry

            lax.fori_loop(0, 4, unpack, 0)
        else:
            landed(4)

            def unpack(j, carry):
                left = pl.multiple_of(j * 256, 256)
                near = srecv[0, :, :, pl.ds(left, 256)].astype(F32)
                far = srecv[1, :, :, pl.ds(left, 256)].astype(F32)
                for side in range(2):
                    cols = pl.ds(left + side * 1024, 256)
                    for out, base in ((xs, 0), (gs, 8)):
                        lo = base + 4 * side
                        both = jnp.concatenate([near[:, lo : lo + 4], far[:, lo : lo + 4]], axis=1)
                        out[rows, cols] = both.reshape(128, 256).astype(BF16)
                return carry

            lax.fori_loop(0, 4, unpack, 0)
        if g == 0:
            for k in range(3):
                weight_copy(k).wait_recv()

        def forward(h, carry):
            wide = pl.ds(pl.multiple_of(h * 2 * HALF, 2 * HALF), 2 * HALF)
            narrow = pl.ds(pl.multiple_of(h * HALF, HALF), HALF)
            pre = jnp.dot(xs[rows, :], wgu[:, wide], preferred_element_type=F32)
            gate, up = pre[:, :HALF], pre[:, HALF:]
            hidden_grad = lax.dot_general(gs[rows, :], wd[narrow, :], NT, preferred_element_type=F32)
            s = jax.nn.sigmoid(gate)
            act = gate * s
            hid[rows, narrow] = (act * up).astype(BF16)
            gate_in = (hidden_grad * up * s * (1.0 + gate * (1.0 - s))).astype(BF16)
            up_in = (hidden_grad * act).astype(BF16)
            giui[rows, wide] = jnp.concatenate([gate_in, up_in], axis=1)
            return carry

        lax.fori_loop(0, 2, forward, 0)

        if g == 3:
            def back_single(j, carry):
                cols = pl.ds(pl.multiple_of(j * 256, 256), 256)
                parts = []
                for q in range(4):
                    feats = pl.ds(pl.multiple_of(j * 256 + q * 512, 256), 256)
                    a = lax.dot_general(giui[rows, :], wgu[feats, :], NT, preferred_element_type=F32)
                    parts.append(a.reshape(16, 8, 256))
                for c in range(2):
                    packed = jnp.concatenate([a[:, c * 4 : c * 4 + 4] for a in parts], axis=1)
                    srsend[c, :, :, cols] = packed.astype(BF16)
                return carry

            lax.fori_loop(0, 2, back_single, 0)
            return

        def back(j, carry):
            out = pl.ds(pl.multiple_of(j * 512, 512), 512)
            right = pl.ds(pl.multiple_of(j * 512 + 1024, 512), 512)
            a = lax.dot_general(giui[rows, :], wgu[out, :], NT, preferred_element_type=F32)
            b = lax.dot_general(giui[rows, :], wgu[right, :], NT, preferred_element_type=F32)
            both = jnp.concatenate([a.reshape(16, 8, 512), b.reshape(16, 8, 512)], axis=1)
            rsend[g, :, :, out] = both.astype(BF16)
            return carry

        lax.fori_loop(0, 2, back, 0)

    def send_back(g):
        def go(i, carry):
            ret(g, i).start()
            return carry

        lax.fori_loop(1, 16, go, 0)
        ret_own(g).start()

    def ways(h, block):
        return (0, 1) if h < 4 else (block // 2,)

    def inward(direction, h, block):
        cols = pl.ds(block * 512, 512)
        if h == 4:
            dst = zhalf.at[:, cols]
        else:
            dst = zrecv.at[direction, h - 1, :, cols]
        return pltpu.make_async_remote_copy(
            src_ref=zsend.at[(UP, DOWN)[direction][h], :, cols], dst_ref=dst,
            send_sem=z_s.at[direction, h - 1, block], recv_sem=z_r.at[direction, h - 1, block],
            device_id=zdev((7, 1)[direction]), device_id_type=MESH,
        )

    def returned(g):
        def wait(i, carry):
            ret_recv(g, i).wait_recv()
            return carry

        lax.fori_loop(1, 16, wait, 0)
        ret_own(g).wait()

    def combine_single(c):
        returned(3 + c)
        for block in (0, 2, 1, 3):
            cols = pl.ds(block * 512, 512)
            part = srrecv[c, :, :, :].astype(F32)[:, block * 4 : block * 4 + 4]
            part = jnp.concatenate([part, part], axis=1).reshape(128, 512).astype(BF16)
            total = jnp.dot(selt[3], part, preferred_element_type=F32)
            if c == 0:
                own[:, cols] = total[:ROWS]
            else:
                zsend[7, :, cols] = total[ROWS : 2 * ROWS].astype(BF16)
                for direction in ways(4, block):
                    inward(direction, 4, block).start()

    def combine(g):
        first, second = PAIRS[g]
        returned(g)
        for block in (0, 2, 1, 3):
            cols = pl.ds(block * 512, 512)
            narrow = pl.ds(block % 2 * 512, 512)
            side = block // 2
            part = rrecv[g, :, :, narrow].astype(F32)[:, side * 8 : side * 8 + 8]
            total = jnp.dot(selt[g], part.reshape(128, 512).astype(BF16), preferred_element_type=F32)
            near, far = total[:ROWS], total[ROWS : 2 * ROWS]
            for direction in ways(g + 2, block):
                inward(direction, g + 2, block).wait_recv()
            if g < 2:
                near = near + zrecv[0, g + 1, :, cols].astype(F32)
                far = far + zrecv[1, g + 1, :, cols].astype(F32)
            elif side == 0:
                near = near + zhalf[:, cols].astype(F32)
            else:
                far = far + zhalf[:, cols].astype(F32)
            zsend[first, :, cols] = near.astype(BF16)
            zsend[second, :, cols] = far.astype(BF16)
            for direction in (0, 1):
                inward(direction, g + 1, block).start()

    def grad_copy(k):
        src, dst = (
            (wgu.at[:, pl.ds(2 * HALF, HALF)], gu_recv.at[0]),
            (wgu.at[:, pl.ds(3 * HALF, HALF)], gu_recv.at[1]),
            (wd.at[pl.ds(HALF, HALF)], d_recv),
        )[k]
        return pltpu.make_async_remote_copy(
            src_ref=src, dst_ref=dst, send_sem=g_s.at[k], recv_sem=g_r.at[k],
            device_id=partner, device_id_type=MESH,
        )

    def gate_up_grads():
        for k in range(3):
            weight_copy(k).wait_send()

        def tile(j, carry):
            rows = pl.ds(pl.multiple_of(j * 256, 256), 256)
            both = lax.dot_general(xs[:, rows], giui[...], TN, preferred_element_type=F32)
            wgu[rows, :] = both.astype(BF16)
            return carry

        lax.fori_loop(0, 8, tile, 0)
        grad_copy(0).start()
        grad_copy(1).start()

    def down_grads():
        def tile_down(j, carry):
            cols = pl.ds(pl.multiple_of(j * 512, 512), 512)
            both = lax.dot_general(hid[...], gs[:, cols], TN, preferred_element_type=F32)
            wd[:, cols] = both.astype(BF16)
            return carry

        lax.fori_loop(0, 4, tile_down, 0)
        grad_copy(2).start()

    def store(k):
        src, dst = (
            (gu_recv.at[0], gate_out), (gu_recv.at[1], up_out), (d_recv, down_out), (result, tok_out)
        )[k]
        return pltpu.make_async_copy(src, dst, store_sem.at[k])

    def add_grads():
        for k in range(2):
            grad_copy(k).wait_recv()

            def tile(j, carry):
                rows = pl.ds(pl.multiple_of(j * 256, 256), 256)
                total = wgu[rows, k * HALF : (k + 1) * HALF].astype(F32) + gu_recv[k, rows, :].astype(F32)
                gu_recv[k, rows, :] = total.astype(BF16)
                return carry

            lax.fori_loop(0, 8, tile, 0)
            store(k).start()
        grad_copy(2).wait_recv()

        def tile_down(j, carry):
            cols = pl.ds(pl.multiple_of(j * 512, 512), 512)
            total = wd[0:HALF, cols].astype(F32) + d_recv[:, cols].astype(F32)
            d_recv[:, cols] = total.astype(BF16)
            return carry

        lax.fori_loop(0, 4, tile_down, 0)
        store(2).start()

    dispatch(3)
    for k in range(3):
        loads[4 + k].wait()
        weight_copy(k).start()
    advance(1, (0, 2))
    near_sel, near_scale = select(1, 2)
    selt[0] = near_sel.T.astype(BF16)
    near_rows = near_sel.astype(BF16)[:, : 2 * ROWS]
    dispatch_near(0, tok, near_rows, None)
    advance(1, (1,))
    dispatch_near(5, grad, near_rows, near_scale)
    advance(2)
    dispatch(1)
    advance(3)
    dispatch(2)
    advance(4)
    dispatch(4)
    selt[3] = select(*PAIRS[3])[0].T.astype(BF16)
    expert_rows(0)
    expert_rows(1)
    expert_rows(2)
    send_back(2)
    expert_rows(3)
    send_back(4)
    send_back(1)
    send_back(0)
    send_back(3)
    gate_up_grads()
    combine_single(1)
    combine(2)
    down_grads()
    combine(1)
    combine(0)
    add_grads()
    combine_single(0)
    for block in (0, 2, 1, 3):
        cols = pl.ds(block * 512, 512)
        for direction in (0, 1):
            inward(direction, 1, block).wait_recv()
        total = own[:, cols] + zrecv[0, 0, :, cols].astype(F32) + zrecv[1, 0, :, cols].astype(F32)
        result[:, cols] = total.astype(BF16)
    store(3).start()

    for h in range(1, 5):
        for direction in (0, 1):
            for piece in pieces(direction, h):
                hop(direction, h, piece).wait_send()
    for k in range(3):
        grad_copy(k).wait_send()
    for h in range(1, 5):
        for block in range(4):
            for direction in ways(h, block):
                inward(direction, h, block).wait_send()

    def drain(i, carry):
        for g in range(6):
            disp(g, i).wait_send()
        for g in range(5):
            ret(g, i).wait_send()
        return carry

    lax.fori_loop(1, 16, drain, 0)
    for k in range(4):
        store(k).wait()


def store_out(*refs):
    sems = refs[8]
    copies = [pltpu.make_async_copy(refs[k], refs[4 + k], sems.at[k]) for k in range(4)]
    for c in copies:
        c.start()
    for c in copies:
        c.wait()


def per_device(tokens, grad_out, expert_ids, gate_probs, gate_weight, up_weight, down_weight):
    anywhere = pl.BlockSpec(memory_space=pl.ANY)
    dma = pltpu.SemaphoreType.DMA
    tok_grad, gate_grad, up_grad, down_grad = pl.pallas_call(
        kernel,
        out_shape=(
            jax.ShapeDtypeStruct((ROWS, D), BF16),
            jax.ShapeDtypeStruct((D, HALF), BF16),
            jax.ShapeDtypeStruct((D, HALF), BF16),
            jax.ShapeDtypeStruct((HALF, D), BF16),
        ),
        in_specs=[pl.BlockSpec(memory_space=pltpu.HBM)] * 7,
        out_specs=[anywhere] * 4,
        scratch_shapes=[
            pltpu.VMEM((TOP, ROWS), jnp.int32),
            pltpu.VMEM((TOP, ROWS), F32),
            pltpu.VMEM((ROWS, D), BF16),
            pltpu.VMEM((REP, ROWS, D), BF16),
            pltpu.VMEM((REP, ROWS, D), BF16),
            pltpu.VMEM((REP, 16, 128), F32),
            pltpu.VMEM((D, 4 * HALF), BF16),
            pltpu.VMEM((2 * HALF, D), BF16),
            pltpu.VMEM((2, 16, 16, D), BF16),
            pltpu.VMEM((2, 16, 16, D), BF16),
            pltpu.VMEM((4, 16, 16, D // 2), BF16),
            pltpu.VMEM((4, 16, 16, D // 2), BF16),
            pltpu.VMEM((GROUPS * 128, D), BF16),
            pltpu.VMEM((GROUPS * 128, D), BF16),
            pltpu.VMEM((GROUPS * 128, 2 * HALF), BF16),
            pltpu.VMEM((GROUPS * 128, 4 * HALF), BF16),
            pltpu.VMEM((3, 16, 16, D // 2), BF16),
            pltpu.VMEM((3, 16, 16, D // 2), BF16),
            pltpu.VMEM((2, 16, 16, D // 4), BF16),
            pltpu.VMEM((2, 16, 16, D // 4), BF16),
            pltpu.VMEM((GROUPS, 128, 128), BF16),
            pltpu.VMEM((REP, ROWS, D), BF16),
            pltpu.VMEM((2, 3, ROWS, D), BF16),
            pltpu.VMEM((ROWS, D), BF16),
            pltpu.VMEM((ROWS, D), F32),
            pltpu.VMEM((2, D, HALF), BF16),
            pltpu.VMEM((HALF, D), BF16),
            dma((7,)),
            dma((4,)),
            dma((2, 4, 3)),
            dma((2, 4, 3)),
            dma((3,)),
            dma((3,)),
            dma((6, 16)),
            dma((6, 16)),
            dma((5, 16)),
            dma((5, 16)),
            dma((2, 4, 4)),
            dma((2, 4, 4)),
            dma((3,)),
            dma((3,)),
        ],
        compiler_params=pltpu.CompilerParams(
            collective_id=0, has_side_effects=True, vmem_limit_bytes=LIMIT * 2**20
        ),
    )(*(
        pltpu.with_memory_space_constraint(x, pltpu.HBM)
        for x in (
            tokens, grad_out, expert_ids.T, gate_probs.T, gate_weight[0], up_weight[0], down_weight[0]
        )
    ))
    outs = (tok_grad, gate_grad, up_grad, down_grad)
    tok_grad, gate_grad, up_grad, down_grad = pl.pallas_call(
        store_out,
        out_shape=tuple(jax.ShapeDtypeStruct(x.shape, x.dtype) for x in outs),
        in_specs=[anywhere] * 4,
        out_specs=[anywhere] * 4,
        scratch_shapes=[dma((4,))],
        compiler_params=pltpu.CompilerParams(vmem_limit_bytes=2**20),
    )(*outs)
    return tok_grad, gate_grad[None], up_grad[None], down_grad[None]


def solution(mesh):
    rows = P(("rep", "exp"), None)
    mats = P(("rep", "exp"), None, None)
    return jax.shard_map(
        per_device,
        mesh=mesh,
        in_specs=(rows, rows, rows, rows, mats, mats, mats),
        out_specs=(rows, mats, mats, mats),
        check_vma=False,
    )
```

```python
import jax
import jax.numpy as jnp
from jax import lax
from jax.experimental import pallas as pl
from jax.experimental.pallas import tpu as pltpu
from jax.sharding import PartitionSpec as P

MESH = pl.DeviceIdType.MESH
F32 = jnp.float32
BF16 = jnp.bfloat16
REP = 8
ROWS = 48
D = 2048
HALF = 384
TOP = 8
GROUPS = 4
LIMIT = 44
NT = (((1,), (1,)), ((), ()))
TN = (((0,), (0,)), ((), ()))


UP = (0, 1, 3, 5, 7)
DOWN = (0, 2, 4, 6, 7)
PAIRS = ((1, 2), (3, 4), (5, 6), (0, 7))


def kernel(
    tok_hbm, grad_hbm, ids_hbm, prob_hbm, gate_hbm, up_hbm, down_hbm,
    tok_out, gate_out, up_out, down_out,
    ids_in, prob_in, result, tok, grad, meta, wgu, wd, send, recv, ssend, srecv, xs, gs, hid, giui, rsend, rrecv, srsend, srrecv, selt,
    zsend, zrecv, zhalf, own, gu_recv, d_recv,
    load_sem, store_sem, ring_s, ring_r, w_s, w_r, disp_s, disp_r, ret_s, ret_r, z_s, z_r, g_s, g_r,
):
    z = lax.axis_index("rep")
    e = lax.axis_index("exp")
    p = e // 2
    core = e % 2
    px = p % 4
    py = p // 4
    partner = (z, p * 2 + 1 - core)

    def plane(i):
        k = (i * 7) % 16
        return ((py + k // 4) % 4) * 4 + (px + k % 4) % 4

    def zdev(d):
        return ((z + d) % REP, e)

    loads = [
        pltpu.make_async_copy(ids_hbm, ids_in, load_sem.at[0]),
        pltpu.make_async_copy(prob_hbm, prob_in, load_sem.at[6]),
        pltpu.make_async_copy(tok_hbm, tok.at[0], load_sem.at[1]),
        pltpu.make_async_copy(grad_hbm, grad.at[0], load_sem.at[2]),
        pltpu.make_async_copy(gate_hbm, wgu.at[:, pl.ds(0, HALF)], load_sem.at[3]),
        pltpu.make_async_copy(up_hbm, wgu.at[:, pl.ds(HALF, HALF)], load_sem.at[4]),
        pltpu.make_async_copy(down_hbm, wd.at[pl.ds(0, HALF)], load_sem.at[5]),
    ]
    for c in loads:
        c.start()

    barrier = pltpu.get_barrier_semaphore()

    def greet_plane(i, carry):
        pl.semaphore_signal(barrier, inc=1, device_id=(z, plane(i) * 2 + core), device_id_type=MESH)
        return carry

    def greet_z(i, carry):
        pl.semaphore_signal(barrier, inc=1, device_id=zdev(i), device_id_type=MESH)
        return carry

    lax.fori_loop(1, 16, greet_plane, 0)
    lax.fori_loop(1, REP, greet_z, 0)
    pl.semaphore_signal(barrier, inc=1, device_id=partner, device_id_type=MESH)
    pl.semaphore_wait(barrier, 23)

    def hop(direction, h, piece):
        table = (UP, DOWN)[direction]
        buf = (tok, grad, meta)[piece]
        return pltpu.make_async_remote_copy(
            src_ref=buf.at[table[h - 1]],
            dst_ref=buf.at[table[h]],
            send_sem=ring_s.at[direction, h - 1, piece],
            recv_sem=ring_r.at[direction, h - 1, piece],
            device_id=zdev((1, 7)[direction]),
            device_id_type=MESH,
        )

    def pieces(direction, h):
        if h < 4:
            return (0, 1, 2)
        return ((0, 2), (1,))[direction]

    for c in loads[2:4]:
        c.wait()
    for direction in (0, 1):
        hop(direction, 1, 0).start()
    for c in loads[:2]:
        c.wait()

    def twice(values, fill):
        return jnp.concatenate([values, values, jnp.full((TOP, 128 - 2 * ROWS), fill, F32)], axis=1)

    meta[0, 0:8, :] = twice(ids_in[...].astype(F32), -1.0)
    meta[0, 8:16, :] = twice(prob_in[...], 0.0)
    for piece in (2, 1):
        for direction in (0, 1):
            hop(direction, 1, piece).start()

    def advance(h, chosen=(0, 2, 1)):
        for piece in chosen:
            for direction in (0, 1):
                if piece in pieces(direction, h):
                    hop(direction, h, piece).wait_recv()
                    if h < 4 and piece in pieces(direction, h + 1):
                        hop(direction, h + 1, piece).start()

    def weight_copy(k):
        if k < 2:
            src = wgu.at[:, pl.ds(k * HALF, HALF)]
            dst = wgu.at[:, pl.ds((k + 2) * HALF, HALF)]
        else:
            src = wd.at[pl.ds(0, HALF)]
            dst = wd.at[pl.ds(HALF, HALF)]
        return pltpu.make_async_remote_copy(
            src_ref=src, dst_ref=dst, send_sem=w_s.at[k], recv_sem=w_r.at[k],
            device_id=partner, device_id_type=MESH,
        )

    row = lax.broadcasted_iota(jnp.int32, (128, 128), 0)
    lane = lax.broadcasted_iota(jnp.int32, (128, 128), 1)
    low = lane < ROWS
    same_chunk = ((row // 4) % 2 == 0) == low
    tri = jnp.where(row < lane, 1.0, 0.0).astype(BF16)
    expert = (16 * z + row // 8).astype(F32)
    rank = (row % 4).astype(F32)

    def disp_refs(g):
        if g in (1, 2):
            return send.at[g - 1], recv.at[g - 1]
        slot = {3: 0, 4: 1, 0: 2, 5: 3}[g]
        return ssend.at[slot], srecv.at[slot]

    def disp(g, i):
        q = plane(i)
        src, dst = disp_refs(g)
        return pltpu.make_async_remote_copy(
            src_ref=src.at[q], dst_ref=dst.at[p],
            send_sem=disp_s.at[g, q], recv_sem=disp_r.at[g, p],
            device_id=(z, q * 2 + core), device_id_type=MESH,
        )

    def disp_own(g):
        src, dst = disp_refs(g)
        return pltpu.make_async_copy(src.at[p], dst.at[p], disp_r.at[g, p])

    def disp_recv(g, i):
        q = plane(i)
        src, dst = disp_refs(g)
        return pltpu.make_async_remote_copy(
            src_ref=src.at[q], dst_ref=dst.at[q],
            send_sem=disp_s.at[g, q], recv_sem=disp_r.at[g, q],
            device_id=(z, q * 2 + core), device_id_type=MESH,
        )

    def select(first, second):
        low8 = low[:8]
        ids = jnp.where(low8, meta[first, 0:8, :], meta[second, 0:8, :])
        prob = jnp.where(low8, meta[first, 8:16, :], meta[second, 8:16, :])
        hit = jnp.zeros((128, 128), F32)
        weight = jnp.zeros((128, 128), F32)
        for k in range(TOP):
            match = ids[k : k + 1, :] == expert
            hit = jnp.where(match, 1.0, hit)
            weight = jnp.where(match, prob[k : k + 1, :], weight)
        hit = jnp.where(same_chunk, hit, 0.0)
        before = jnp.dot(hit.astype(BF16), tri, preferred_element_type=F32)
        sel = jnp.where(before == rank, hit, 0.0)
        return sel, jnp.sum(sel * weight, axis=1, keepdims=True)

    def launch(g):
        def go(i, carry):
            disp(g, i).start()
            return carry

        lax.fori_loop(1, 16, go, 0)
        disp_own(g).start()

    def dispatch(g):
        single = g >= 3
        first, second = PAIRS[g] if not single else ((0, 0), (7, 7))[g - 3]
        sel, scale = select(first, second)
        if not single:
            selt[g] = sel.T.astype(BF16)
        sel_rows = sel.astype(BF16)[:, : 2 * ROWS]

        def tile(j, carry):
            cols = pl.ds(pl.multiple_of(j * 512, 512), 512)
            if single:
                right = pl.ds(pl.multiple_of(j * 512 + 1024, 512), 512)
                t2 = jnp.concatenate([tok[first, :, cols], tok[first, :, right]], axis=0)
                g2 = jnp.concatenate([grad[first, :, cols], grad[first, :, right]], axis=0)
            else:
                t2 = tok[first : first + 2, :, cols].reshape(2 * ROWS, 512)
                g2 = grad[first : first + 2, :, cols].reshape(2 * ROWS, 512)
            a = jnp.dot(sel_rows, t2, preferred_element_type=F32)
            b = jnp.dot(sel_rows, g2, preferred_element_type=F32) * scale
            both = jnp.concatenate([a.reshape(16, 8, 512), b.reshape(16, 8, 512)], axis=1)
            disp_refs(g)[0][:, :, cols] = both.astype(BF16)
            return carry

        lax.fori_loop(0, 2 if single else 4, tile, 0)
        launch(g)

    def dispatch_near(message, buf, sel_rows, scale):
        def tile(j, carry):
            cols = pl.ds(pl.multiple_of(j * 512, 512), 512)
            halves = []
            for side in range(2):
                from_cols = pl.ds(pl.multiple_of(j * 512 + side * 1024, 512), 512)
                rows2 = buf[1:3, :, from_cols].reshape(2 * ROWS, 512)
                part = jnp.dot(sel_rows, rows2, preferred_element_type=F32)
                if scale is not None:
                    part = part * scale
                halves.append(part.reshape(16, 8, 512))
            disp_refs(message)[0][:, :, cols] = jnp.concatenate(halves, axis=1).astype(BF16)
            return carry

        lax.fori_loop(0, 2, tile, 0)
        launch(message)

    def ret_refs(g):
        if g < 3:
            return rsend.at[g], rrecv.at[g]
        return srsend.at[g - 3], srrecv.at[g - 3]

    def ret(g, i):
        q = plane(i)
        src, dst = ret_refs(g)
        return pltpu.make_async_remote_copy(
            src_ref=src.at[q], dst_ref=dst.at[p],
            send_sem=ret_s.at[g, q], recv_sem=ret_r.at[g, p],
            device_id=(z, q * 2 + core), device_id_type=MESH,
        )

    def ret_own(g):
        src, dst = ret_refs(g)
        return pltpu.make_async_copy(src.at[p], dst.at[p], ret_r.at[g, p])

    def ret_recv(g, i):
        q = plane(i)
        src, dst = ret_refs(g)
        return pltpu.make_async_remote_copy(
            src_ref=src.at[q], dst_ref=dst.at[q],
            send_sem=ret_s.at[g, q], recv_sem=ret_r.at[g, q],
            device_id=(z, q * 2 + core), device_id_type=MESH,
        )

    def landed(g):
        def wait(i, carry):
            disp_recv(g, i).wait_recv()
            return carry

        lax.fori_loop(1, 16, wait, 0)
        disp_own(g).wait()

    def expert_rows(g):
        rows = pl.ds(g * 128, 128)
        landed(g)
        if g == 0:
            landed(5)

            def unpack(j, carry):
                left = pl.multiple_of(j * 512, 512)
                for slot, out in ((2, xs), (3, gs)):
                    both = srecv[slot, :, :, pl.ds(left, 512)].astype(F32)
                    out[rows, pl.ds(left, 512)] = both[:, 0:8].reshape(128, 512).astype(BF16)
                    out[rows, pl.ds(left + 1024, 512)] = both[:, 8:16].reshape(128, 512).astype(BF16)
                return carry

            lax.fori_loop(0, 2, unpack, 0)
        elif g < 3:
            def unpack(j, carry):
                cols = pl.ds(pl.multiple_of(j * 512, 512), 512)
                both = recv[g - 1, :, :, cols].astype(F32)
                xs[rows, cols] = both[:, 0:8].reshape(128, 512).astype(BF16)
                gs[rows, cols] = both[:, 8:16].reshape(128, 512).astype(BF16)
                return carry

            lax.fori_loop(0, 4, unpack, 0)
        else:
            landed(4)

            def unpack(j, carry):
                left = pl.multiple_of(j * 256, 256)
                near = srecv[0, :, :, pl.ds(left, 256)].astype(F32)
                far = srecv[1, :, :, pl.ds(left, 256)].astype(F32)
                for side in range(2):
                    cols = pl.ds(left + side * 1024, 256)
                    for out, base in ((xs, 0), (gs, 8)):
                        lo = base + 4 * side
                        both = jnp.concatenate([near[:, lo : lo + 4], far[:, lo : lo + 4]], axis=1)
                        out[rows, cols] = both.reshape(128, 256).astype(BF16)
                return carry

            lax.fori_loop(0, 4, unpack, 0)
        if g == 0:
            for k in range(3):
                weight_copy(k).wait_recv()

        def forward(h, carry):
            wide = pl.ds(pl.multiple_of(h * 2 * HALF, 2 * HALF), 2 * HALF)
            narrow = pl.ds(pl.multiple_of(h * HALF, HALF), HALF)
            pre = jnp.dot(xs[rows, :], wgu[:, wide], preferred_element_type=F32)
            gate, up = pre[:, :HALF], pre[:, HALF:]
            hidden_grad = lax.dot_general(gs[rows, :], wd[narrow, :], NT, preferred_element_type=F32)
            s = jax.nn.sigmoid(gate)
            act = gate * s
            hid[rows, narrow] = (act * up).astype(BF16)
            gate_in = (hidden_grad * up * s * (1.0 + gate * (1.0 - s))).astype(BF16)
            up_in = (hidden_grad * act).astype(BF16)
            giui[rows, wide] = jnp.concatenate([gate_in, up_in], axis=1)
            return carry

        lax.fori_loop(0, 2, forward, 0)

        if g == 3:
            def back_single(j, carry):
                cols = pl.ds(pl.multiple_of(j * 256, 256), 256)
                parts = []
                for q in range(4):
                    feats = pl.ds(pl.multiple_of(j * 256 + q * 512, 256), 256)
                    a = lax.dot_general(giui[rows, :], wgu[feats, :], NT, preferred_element_type=F32)
                    parts.append(a.reshape(16, 8, 256))
                for c in range(2):
                    packed = jnp.concatenate([a[:, c * 4 : c * 4 + 4] for a in parts], axis=1)
                    srsend[c, :, :, cols] = packed.astype(BF16)
                return carry

            lax.fori_loop(0, 2, back_single, 0)
            return

        def back(j, carry):
            out = pl.ds(pl.multiple_of(j * 512, 512), 512)
            right = pl.ds(pl.multiple_of(j * 512 + 1024, 512), 512)
            a = lax.dot_general(giui[rows, :], wgu[out, :], NT, preferred_element_type=F32)
            b = lax.dot_general(giui[rows, :], wgu[right, :], NT, preferred_element_type=F32)
            both = jnp.concatenate([a.reshape(16, 8, 512), b.reshape(16, 8, 512)], axis=1)
            rsend[g, :, :, out] = both.astype(BF16)
            return carry

        lax.fori_loop(0, 2, back, 0)

    def send_back(g):
        def go(i, carry):
            ret(g, i).start()
            return carry

        lax.fori_loop(1, 16, go, 0)
        ret_own(g).start()

    def ways(h, block):
        return (0, 1) if h < 4 else (block // 2,)

    def inward(direction, h, block):
        cols = pl.ds(block * 512, 512)
        if h == 4:
            dst = zhalf.at[:, cols]
        else:
            dst = zrecv.at[direction, h - 1, :, cols]
        return pltpu.make_async_remote_copy(
            src_ref=zsend.at[(UP, DOWN)[direction][h], :, cols], dst_ref=dst,
            send_sem=z_s.at[direction, h - 1, block], recv_sem=z_r.at[direction, h - 1, block],
            device_id=zdev((7, 1)[direction]), device_id_type=MESH,
        )

    def returned(g):
        def wait(i, carry):
            ret_recv(g, i).wait_recv()
            return carry

        lax.fori_loop(1, 16, wait, 0)
        ret_own(g).wait()

    def combine_single(c):
        returned(3 + c)
        for block in (0, 2, 1, 3):
            cols = pl.ds(block * 512, 512)
            part = srrecv[c, :, :, :].astype(F32)[:, block * 4 : block * 4 + 4]
            part = jnp.concatenate([part, part], axis=1).reshape(128, 512).astype(BF16)
            total = jnp.dot(selt[3], part, preferred_element_type=F32)
            if c == 0:
                own[:, cols] = total[:ROWS]
            else:
                zsend[7, :, cols] = total[ROWS : 2 * ROWS].astype(BF16)
                for direction in ways(4, block):
                    inward(direction, 4, block).start()

    def combine(g):
        first, second = PAIRS[g]
        returned(g)
        for block in (0, 2, 1, 3):
            cols = pl.ds(block * 512, 512)
            narrow = pl.ds(block % 2 * 512, 512)
            side = block // 2
            part = rrecv[g, :, :, narrow].astype(F32)[:, side * 8 : side * 8 + 8]
            total = jnp.dot(selt[g], part.reshape(128, 512).astype(BF16), preferred_element_type=F32)
            near, far = total[:ROWS], total[ROWS : 2 * ROWS]
            for direction in ways(g + 2, block):
                inward(direction, g + 2, block).wait_recv()
            if g < 2:
                near = near + zrecv[0, g + 1, :, cols].astype(F32)
                far = far + zrecv[1, g + 1, :, cols].astype(F32)
            elif side == 0:
                near = near + zhalf[:, cols].astype(F32)
            else:
                far = far + zhalf[:, cols].astype(F32)
            zsend[first, :, cols] = near.astype(BF16)
            zsend[second, :, cols] = far.astype(BF16)
            for direction in (0, 1):
                inward(direction, g + 1, block).start()

    def grad_copy(k):
        src, dst = (
            (wgu.at[:, pl.ds(2 * HALF, HALF)], gu_recv.at[0]),
            (wgu.at[:, pl.ds(3 * HALF, HALF)], gu_recv.at[1]),
            (wd.at[pl.ds(HALF, HALF)], d_recv),
        )[k]
        return pltpu.make_async_remote_copy(
            src_ref=src, dst_ref=dst, send_sem=g_s.at[k], recv_sem=g_r.at[k],
            device_id=partner, device_id_type=MESH,
        )

    def gate_up_grads():
        for k in range(3):
            weight_copy(k).wait_send()

        def tile(j, carry):
            rows = pl.ds(pl.multiple_of(j * 256, 256), 256)
            both = lax.dot_general(xs[:, rows], giui[...], TN, preferred_element_type=F32)
            wgu[rows, :] = both.astype(BF16)
            return carry

        lax.fori_loop(0, 8, tile, 0)
        grad_copy(0).start()
        grad_copy(1).start()

    def down_grads():
        def tile_down(j, carry):
            cols = pl.ds(pl.multiple_of(j * 512, 512), 512)
            both = lax.dot_general(hid[...], gs[:, cols], TN, preferred_element_type=F32)
            wd[:, cols] = both.astype(BF16)
            return carry

        lax.fori_loop(0, 4, tile_down, 0)
        grad_copy(2).start()

    def store(k):
        src, dst = (
            (gu_recv.at[0], gate_out), (gu_recv.at[1], up_out), (d_recv, down_out), (result, tok_out)
        )[k]
        return pltpu.make_async_copy(src, dst, store_sem.at[k])

    def add_grads():
        for k in range(2):
            grad_copy(k).wait_recv()

            def tile(j, carry):
                rows = pl.ds(pl.multiple_of(j * 256, 256), 256)
                total = wgu[rows, k * HALF : (k + 1) * HALF].astype(F32) + gu_recv[k, rows, :].astype(F32)
                gu_recv[k, rows, :] = total.astype(BF16)
                return carry

            lax.fori_loop(0, 8, tile, 0)
            store(k).start()
        grad_copy(2).wait_recv()

        def tile_down(j, carry):
            cols = pl.ds(pl.multiple_of(j * 512, 512), 512)
            total = wd[0:HALF, cols].astype(F32) + d_recv[:, cols].astype(F32)
            d_recv[:, cols] = total.astype(BF16)
            return carry

        lax.fori_loop(0, 4, tile_down, 0)
        store(2).start()

    dispatch(3)
    for k in range(3):
        loads[4 + k].wait()
        weight_copy(k).start()
    advance(1, (0, 2))
    near_sel, near_scale = select(1, 2)
    selt[0] = near_sel.T.astype(BF16)
    near_rows = near_sel.astype(BF16)[:, : 2 * ROWS]
    dispatch_near(0, tok, near_rows, None)
    advance(1, (1,))
    dispatch_near(5, grad, near_rows, near_scale)
    advance(2)
    dispatch(1)
    advance(3)
    dispatch(2)
    advance(4)
    dispatch(4)
    selt[3] = select(*PAIRS[3])[0].T.astype(BF16)
    expert_rows(0)
    expert_rows(1)
    expert_rows(2)
    send_back(2)
    expert_rows(3)
    send_back(4)
    send_back(1)
    send_back(0)
    send_back(3)
    gate_up_grads()
    combine_single(1)
    combine(2)
    down_grads()
    combine(1)
    combine(0)
    add_grads()
    combine_single(0)
    for block in (0, 2, 1, 3):
        cols = pl.ds(block * 512, 512)
        for direction in (0, 1):
            inward(direction, 1, block).wait_recv()
        total = own[:, cols] + zrecv[0, 0, :, cols].astype(F32) + zrecv[1, 0, :, cols].astype(F32)
        result[:, cols] = total.astype(BF16)
    store(3).start()

    for h in range(1, 5):
        for direction in (0, 1):
            for piece in pieces(direction, h):
                hop(direction, h, piece).wait_send()
    for k in range(3):
        grad_copy(k).wait_send()
    for h in range(1, 5):
        for block in range(4):
            for direction in ways(h, block):
                inward(direction, h, block).wait_send()

    def drain(i, carry):
        for g in range(6):
            disp(g, i).wait_send()
        for g in range(5):
            ret(g, i).wait_send()
        return carry

    lax.fori_loop(1, 16, drain, 0)
    for k in range(4):
        store(k).wait()


def store_out(*refs):
    sems = refs[8]
    copies = [pltpu.make_async_copy(refs[k], refs[4 + k], sems.at[k]) for k in range(4)]
    for c in copies:
        c.start()
    for c in copies:
        c.wait()


def per_device(tokens, grad_out, expert_ids, gate_probs, gate_weight, up_weight, down_weight):
    anywhere = pl.BlockSpec(memory_space=pl.ANY)
    dma = pltpu.SemaphoreType.DMA
    tok_grad, gate_grad, up_grad, down_grad = pl.pallas_call(
        kernel,
        out_shape=(
            jax.ShapeDtypeStruct((ROWS, D), BF16),
            jax.ShapeDtypeStruct((D, HALF), BF16),
            jax.ShapeDtypeStruct((D, HALF), BF16),
            jax.ShapeDtypeStruct((HALF, D), BF16),
        ),
        in_specs=[pl.BlockSpec(memory_space=pltpu.HBM)] * 7,
        out_specs=[anywhere] * 4,
        scratch_shapes=[
            pltpu.VMEM((TOP, ROWS), jnp.int32),
            pltpu.VMEM((TOP, ROWS), F32),
            pltpu.VMEM((ROWS, D), BF16),
            pltpu.VMEM((REP, ROWS, D), BF16),
            pltpu.VMEM((REP, ROWS, D), BF16),
            pltpu.VMEM((REP, 16, 128), F32),
            pltpu.VMEM((D, 4 * HALF), BF16),
            pltpu.VMEM((2 * HALF, D), BF16),
            pltpu.VMEM((2, 16, 16, D), BF16),
            pltpu.VMEM((2, 16, 16, D), BF16),
            pltpu.VMEM((4, 16, 16, D // 2), BF16),
            pltpu.VMEM((4, 16, 16, D // 2), BF16),
            pltpu.VMEM((GROUPS * 128, D), BF16),
            pltpu.VMEM((GROUPS * 128, D), BF16),
            pltpu.VMEM((GROUPS * 128, 2 * HALF), BF16),
            pltpu.VMEM((GROUPS * 128, 4 * HALF), BF16),
            pltpu.VMEM((3, 16, 16, D // 2), BF16),
            pltpu.VMEM((3, 16, 16, D // 2), BF16),
            pltpu.VMEM((2, 16, 16, D // 4), BF16),
            pltpu.VMEM((2, 16, 16, D // 4), BF16),
            pltpu.VMEM((GROUPS, 128, 128), BF16),
            pltpu.VMEM((REP, ROWS, D), BF16),
            pltpu.VMEM((2, 3, ROWS, D), BF16),
            pltpu.VMEM((ROWS, D), BF16),
            pltpu.VMEM((ROWS, D), F32),
            pltpu.VMEM((2, D, HALF), BF16),
            pltpu.VMEM((HALF, D), BF16),
            dma((7,)),
            dma((4,)),
            dma((2, 4, 3)),
            dma((2, 4, 3)),
            dma((3,)),
            dma((3,)),
            dma((6, 16)),
            dma((6, 16)),
            dma((5, 16)),
            dma((5, 16)),
            dma((2, 4, 4)),
            dma((2, 4, 4)),
            dma((3,)),
            dma((3,)),
        ],
        compiler_params=pltpu.CompilerParams(
            collective_id=0, has_side_effects=True, vmem_limit_bytes=LIMIT * 2**20
        ),
    )(*(
        pltpu.with_memory_space_constraint(x, pltpu.HBM)
        for x in (
            tokens, grad_out, expert_ids.T, gate_probs.T, gate_weight[0], up_weight[0], down_weight[0]
        )
    ))
    outs = (tok_grad, gate_grad, up_grad, down_grad)
    tok_grad, gate_grad, up_grad, down_grad = pl.pallas_call(
        store_out,
        out_shape=tuple(jax.ShapeDtypeStruct(x.shape, x.dtype) for x in outs),
        in_specs=[anywhere] * 4,
        out_specs=[anywhere] * 4,
        scratch_shapes=[dma((4,))],
        compiler_params=pltpu.CompilerParams(vmem_limit_bytes=2**20),
    )(*outs)
    return tok_grad, gate_grad[None], up_grad[None], down_grad[None]


def solution(mesh):
    rows = P(("rep", "exp"), None)
    mats = P(("rep", "exp"), None, None)
    return jax.shard_map(
        per_device,
        mesh=mesh,
        in_specs=(rows, rows, rows, rows, mats, mats, mats),
        out_specs=(rows, mats, mats, mats),
        check_vma=False,
    )
```

```python
import jax
import jax.numpy as jnp
from jax import lax
from jax.experimental import pallas as pl
from jax.experimental.pallas import tpu as pltpu
from jax.sharding import PartitionSpec as P

MESH = pl.DeviceIdType.MESH
F32 = jnp.float32
BF16 = jnp.bfloat16
REP = 8
ROWS = 48
D = 2048
HALF = 384
TOP = 8
GROUPS = 4
LIMIT = 44
NT = (((1,), (1,)), ((), ()))
TN = (((0,), (0,)), ((), ()))


UP = (0, 1, 3, 5, 7)
DOWN = (0, 2, 4, 6, 7)
PAIRS = ((1, 2), (3, 4), (5, 6), (0, 7))


def kernel(
    tok_hbm, grad_hbm, ids_hbm, prob_hbm, gate_hbm, up_hbm, down_hbm,
    tok_out, gate_out, up_out, down_out,
    ids_in, prob_in, result, tok, grad, meta, wgu, wd, send, recv, ssend, srecv, xs, gs, hid, giui, rsend, rrecv, srsend, srrecv, selt,
    zsend, zrecv, zhalf, own, gu_recv, d_recv,
    load_sem, store_sem, ring_s, ring_r, w_s, w_r, disp_s, disp_r, ret_s, ret_r, z_s, z_r, g_s, g_r,
):
    z = lax.axis_index("rep")
    e = lax.axis_index("exp")
    p = e // 2
    core = e % 2
    px = p % 4
    py = p // 4
    partner = (z, p * 2 + 1 - core)

    def plane(i):
        return ((py + i // 4) % 4) * 4 + (px + i % 4) % 4

    def zdev(d):
        return ((z + d) % REP, e)

    loads = [
        pltpu.make_async_copy(ids_hbm, ids_in, load_sem.at[0]),
        pltpu.make_async_copy(prob_hbm, prob_in, load_sem.at[6]),
        pltpu.make_async_copy(tok_hbm, tok.at[0], load_sem.at[1]),
        pltpu.make_async_copy(grad_hbm, grad.at[0], load_sem.at[2]),
        pltpu.make_async_copy(gate_hbm, wgu.at[:, pl.ds(0, HALF)], load_sem.at[3]),
        pltpu.make_async_copy(up_hbm, wgu.at[:, pl.ds(HALF, HALF)], load_sem.at[4]),
        pltpu.make_async_copy(down_hbm, wd.at[pl.ds(0, HALF)], load_sem.at[5]),
    ]
    for c in loads:
        c.start()

    barrier = pltpu.get_barrier_semaphore()

    def greet_plane(i, carry):
        pl.semaphore_signal(barrier, inc=1, device_id=(z, plane(i) * 2 + core), device_id_type=MESH)
        return carry

    def greet_z(i, carry):
        pl.semaphore_signal(barrier, inc=1, device_id=zdev(i), device_id_type=MESH)
        return carry

    lax.fori_loop(1, 16, greet_plane, 0)
    lax.fori_loop(1, REP, greet_z, 0)
    pl.semaphore_signal(barrier, inc=1, device_id=partner, device_id_type=MESH)
    pl.semaphore_wait(barrier, 23)

    def hop(direction, h, piece):
        table = (UP, DOWN)[direction]
        buf = (tok, grad, meta)[piece]
        return pltpu.make_async_remote_copy(
            src_ref=buf.at[table[h - 1]],
            dst_ref=buf.at[table[h]],
            send_sem=ring_s.at[direction, h - 1, piece],
            recv_sem=ring_r.at[direction, h - 1, piece],
            device_id=zdev((1, 7)[direction]),
            device_id_type=MESH,
        )

    def pieces(direction, h):
        if h < 4:
            return (0, 1, 2)
        return ((0, 2), (1,))[direction]

    for c in loads[2:4]:
        c.wait()
    for direction in (0, 1):
        hop(direction, 1, 0).start()
    for c in loads[:2]:
        c.wait()

    def twice(values, fill):
        return jnp.concatenate([values, values, jnp.full((TOP, 128 - 2 * ROWS), fill, F32)], axis=1)

    meta[0, 0:8, :] = twice(ids_in[...].astype(F32), -1.0)
    meta[0, 8:16, :] = twice(prob_in[...], 0.0)
    for piece in (2, 1):
        for direction in (0, 1):
            hop(direction, 1, piece).start()

    def advance(h, chosen=(0, 2, 1)):
        for piece in chosen:
            for direction in (0, 1):
                if piece in pieces(direction, h):
                    hop(direction, h, piece).wait_recv()
                    if h < 4 and piece in pieces(direction, h + 1):
                        hop(direction, h + 1, piece).start()

    def weight_copy(k):
        if k < 2:
            src = wgu.at[:, pl.ds(k * HALF, HALF)]
            dst = wgu.at[:, pl.ds((k + 2) * HALF, HALF)]
        else:
            src = wd.at[pl.ds(0, HALF)]
            dst = wd.at[pl.ds(HALF, HALF)]
        return pltpu.make_async_remote_copy(
            src_ref=src, dst_ref=dst, send_sem=w_s.at[k], recv_sem=w_r.at[k],
            device_id=partner, device_id_type=MESH,
        )

    row = lax.broadcasted_iota(jnp.int32, (128, 128), 0)
    lane = lax.broadcasted_iota(jnp.int32, (128, 128), 1)
    low = lane < ROWS
    same_chunk = ((row // 4) % 2 == 0) == low
    tri = jnp.where(row < lane, 1.0, 0.0).astype(BF16)
    expert = (16 * z + row // 8).astype(F32)
    rank = (row % 4).astype(F32)

    def disp_refs(g):
        if g in (1, 2):
            return send.at[g - 1], recv.at[g - 1]
        slot = {3: 0, 4: 1, 0: 2, 5: 3}[g]
        return ssend.at[slot], srecv.at[slot]

    def disp(g, i):
        q = plane(i)
        src, dst = disp_refs(g)
        return pltpu.make_async_remote_copy(
            src_ref=src.at[q], dst_ref=dst.at[p],
            send_sem=disp_s.at[g, q], recv_sem=disp_r.at[g, p],
            device_id=(z, q * 2 + core), device_id_type=MESH,
        )

    def disp_own(g):
        src, dst = disp_refs(g)
        return pltpu.make_async_copy(src.at[p], dst.at[p], disp_r.at[g, p])

    def disp_recv(g, i):
        q = plane(i)
        src, dst = disp_refs(g)
        return pltpu.make_async_remote_copy(
            src_ref=src.at[q], dst_ref=dst.at[q],
            send_sem=disp_s.at[g, q], recv_sem=disp_r.at[g, q],
            device_id=(z, q * 2 + core), device_id_type=MESH,
        )

    def select(first, second):
        low8 = low[:8]
        ids = jnp.where(low8, meta[first, 0:8, :], meta[second, 0:8, :])
        prob = jnp.where(low8, meta[first, 8:16, :], meta[second, 8:16, :])
        hit = jnp.zeros((128, 128), F32)
        weight = jnp.zeros((128, 128), F32)
        for k in range(TOP):
            match = ids[k : k + 1, :] == expert
            hit = jnp.where(match, 1.0, hit)
            weight = jnp.where(match, prob[k : k + 1, :], weight)
        hit = jnp.where(same_chunk, hit, 0.0)
        before = jnp.dot(hit.astype(BF16), tri, preferred_element_type=F32)
        sel = jnp.where(before == rank, hit, 0.0)
        return sel, jnp.sum(sel * weight, axis=1, keepdims=True)

    def launch(g):
        def go(i, carry):
            disp(g, i).start()
            return carry

        lax.fori_loop(1, 16, go, 0)
        disp_own(g).start()

    def dispatch(g):
        single = g >= 3
        first, second = PAIRS[g] if not single else ((0, 0), (7, 7))[g - 3]
        sel, scale = select(first, second)
        if not single:
            selt[g] = sel.T.astype(BF16)
        sel_rows = sel.astype(BF16)[:, : 2 * ROWS]

        def tile(j, carry):
            cols = pl.ds(pl.multiple_of(j * 512, 512), 512)
            if single:
                right = pl.ds(pl.multiple_of(j * 512 + 1024, 512), 512)
                t2 = jnp.concatenate([tok[first, :, cols], tok[first, :, right]], axis=0)
                g2 = jnp.concatenate([grad[first, :, cols], grad[first, :, right]], axis=0)
            else:
                t2 = tok[first : first + 2, :, cols].reshape(2 * ROWS, 512)
                g2 = grad[first : first + 2, :, cols].reshape(2 * ROWS, 512)
            a = jnp.dot(sel_rows, t2, preferred_element_type=F32)
            b = jnp.dot(sel_rows, g2, preferred_element_type=F32) * scale
            both = jnp.concatenate([a.reshape(16, 8, 512), b.reshape(16, 8, 512)], axis=1)
            disp_refs(g)[0][:, :, cols] = both.astype(BF16)
            return carry

        lax.fori_loop(0, 2 if single else 4, tile, 0)
        launch(g)

    def dispatch_near(message, buf, sel_rows, scale):
        def tile(j, carry):
            cols = pl.ds(pl.multiple_of(j * 512, 512), 512)
            halves = []
            for side in range(2):
                from_cols = pl.ds(pl.multiple_of(j * 512 + side * 1024, 512), 512)
                rows2 = buf[1:3, :, from_cols].reshape(2 * ROWS, 512)
                part = jnp.dot(sel_rows, rows2, preferred_element_type=F32)
                if scale is not None:
                    part = part * scale
                halves.append(part.reshape(16, 8, 512))
            disp_refs(message)[0][:, :, cols] = jnp.concatenate(halves, axis=1).astype(BF16)
            return carry

        lax.fori_loop(0, 2, tile, 0)
        launch(message)

    def ret_refs(g):
        if g < 3:
            return rsend.at[g], rrecv.at[g]
        return srsend.at[g - 3], srrecv.at[g - 3]

    def ret(g, i):
        q = plane(i)
        src, dst = ret_refs(g)
        return pltpu.make_async_remote_copy(
            src_ref=src.at[q], dst_ref=dst.at[p],
            send_sem=ret_s.at[g, q], recv_sem=ret_r.at[g, p],
            device_id=(z, q * 2 + core), device_id_type=MESH,
        )

    def ret_own(g):
        src, dst = ret_refs(g)
        return pltpu.make_async_copy(src.at[p], dst.at[p], ret_r.at[g, p])

    def ret_recv(g, i):
        q = plane(i)
        src, dst = ret_refs(g)
        return pltpu.make_async_remote_copy(
            src_ref=src.at[q], dst_ref=dst.at[q],
            send_sem=ret_s.at[g, q], recv_sem=ret_r.at[g, q],
            device_id=(z, q * 2 + core), device_id_type=MESH,
        )

    def landed(g):
        def wait(i, carry):
            disp_recv(g, i).wait_recv()
            return carry

        lax.fori_loop(1, 16, wait, 0)
        disp_own(g).wait()

    def expert_rows(g):
        rows = pl.ds(g * 128, 128)
        landed(g)
        if g == 0:
            landed(5)

            def unpack(j, carry):
                left = pl.multiple_of(j * 512, 512)
                for slot, out in ((2, xs), (3, gs)):
                    both = srecv[slot, :, :, pl.ds(left, 512)].astype(F32)
                    out[rows, pl.ds(left, 512)] = both[:, 0:8].reshape(128, 512).astype(BF16)
                    out[rows, pl.ds(left + 1024, 512)] = both[:, 8:16].reshape(128, 512).astype(BF16)
                return carry

            lax.fori_loop(0, 2, unpack, 0)
        elif g < 3:
            def unpack(j, carry):
                cols = pl.ds(pl.multiple_of(j * 512, 512), 512)
                both = recv[g - 1, :, :, cols].astype(F32)
                xs[rows, cols] = both[:, 0:8].reshape(128, 512).astype(BF16)
                gs[rows, cols] = both[:, 8:16].reshape(128, 512).astype(BF16)
                return carry

            lax.fori_loop(0, 4, unpack, 0)
        else:
            landed(4)

            def unpack(j, carry):
                left = pl.multiple_of(j * 256, 256)
                near = srecv[0, :, :, pl.ds(left, 256)].astype(F32)
                far = srecv[1, :, :, pl.ds(left, 256)].astype(F32)
                for side in range(2):
                    cols = pl.ds(left + side * 1024, 256)
                    for out, base in ((xs, 0), (gs, 8)):
                        lo = base + 4 * side
                        both = jnp.concatenate([near[:, lo : lo + 4], far[:, lo : lo + 4]], axis=1)
                        out[rows, cols] = both.reshape(128, 256).astype(BF16)
                return carry

            lax.fori_loop(0, 4, unpack, 0)
        if g == 0:
            for k in range(3):
                weight_copy(k).wait_recv()

        def forward(h, carry):
            wide = pl.ds(pl.multiple_of(h * 2 * HALF, 2 * HALF), 2 * HALF)
            narrow = pl.ds(pl.multiple_of(h * HALF, HALF), HALF)
            pre = jnp.dot(xs[rows, :], wgu[:, wide], preferred_element_type=F32)
            gate, up = pre[:, :HALF], pre[:, HALF:]
            hidden_grad = lax.dot_general(gs[rows, :], wd[narrow, :], NT, preferred_element_type=F32)
            s = jax.nn.sigmoid(gate)
            act = gate * s
            hid[rows, narrow] = (act * up).astype(BF16)
            gate_in = (hidden_grad * up * s * (1.0 + gate * (1.0 - s))).astype(BF16)
            up_in = (hidden_grad * act).astype(BF16)
            giui[rows, wide] = jnp.concatenate([gate_in, up_in], axis=1)
            return carry

        lax.fori_loop(0, 2, forward, 0, unroll=True)

        if g == 3:
            def back_single(j, carry):
                cols = pl.ds(pl.multiple_of(j * 256, 256), 256)
                parts = []
                for q in range(4):
                    feats = pl.ds(pl.multiple_of(j * 256 + q * 512, 256), 256)
                    a = lax.dot_general(giui[rows, :], wgu[feats, :], NT, preferred_element_type=F32)
                    parts.append(a.reshape(16, 8, 256))
                for c in range(2):
                    packed = jnp.concatenate([a[:, c * 4 : c * 4 + 4] for a in parts], axis=1)
                    srsend[c, :, :, cols] = packed.astype(BF16)
                return carry

            lax.fori_loop(0, 2, back_single, 0, unroll=True)
            return

        def back(j, carry):
            out = pl.ds(pl.multiple_of(j * 512, 512), 512)
            right = pl.ds(pl.multiple_of(j * 512 + 1024, 512), 512)
            a = lax.dot_general(giui[rows, :], wgu[out, :], NT, preferred_element_type=F32)
            b = lax.dot_general(giui[rows, :], wgu[right, :], NT, preferred_element_type=F32)
            both = jnp.concatenate([a.reshape(16, 8, 512), b.reshape(16, 8, 512)], axis=1)
            rsend[g, :, :, out] = both.astype(BF16)
            return carry

        lax.fori_loop(0, 2, back, 0, unroll=True)

    def send_back(g):
        def go(i, carry):
            ret(g, i).start()
            return carry

        lax.fori_loop(1, 16, go, 0)
        ret_own(g).start()

    def ways(h, block):
        return (0, 1) if h < 4 else (block // 2,)

    def inward(direction, h, block):
        cols = pl.ds(block * 512, 512)
        if h == 4:
            dst = zhalf.at[:, cols]
        else:
            dst = zrecv.at[direction, h - 1, :, cols]
        return pltpu.make_async_remote_copy(
            src_ref=zsend.at[(UP, DOWN)[direction][h], :, cols], dst_ref=dst,
            send_sem=z_s.at[direction, h - 1, block], recv_sem=z_r.at[direction, h - 1, block],
            device_id=zdev((7, 1)[direction]), device_id_type=MESH,
        )

    def returned(g):
        def wait(i, carry):
            ret_recv(g, i).wait_recv()
            return carry

        lax.fori_loop(1, 16, wait, 0)
        ret_own(g).wait()

    def combine_single(c):
        returned(3 + c)
        for block in (0, 2, 1, 3):
            cols = pl.ds(block * 512, 512)
            part = srrecv[c, :, :, :].astype(F32)[:, block * 4 : block * 4 + 4]
            part = jnp.concatenate([part, part], axis=1).reshape(128, 512).astype(BF16)
            total = jnp.dot(selt[3], part, preferred_element_type=F32)
            if c == 0:
                own[:, cols] = total[:ROWS]
            else:
                zsend[7, :, cols] = total[ROWS : 2 * ROWS].astype(BF16)
                for direction in ways(4, block):
                    inward(direction, 4, block).start()

    def combine(g):
        first, second = PAIRS[g]
        returned(g)
        for block in (0, 2, 1, 3):
            cols = pl.ds(block * 512, 512)
            narrow = pl.ds(block % 2 * 512, 512)
            side = block // 2
            part = rrecv[g, :, :, narrow].astype(F32)[:, side * 8 : side * 8 + 8]
            total = jnp.dot(selt[g], part.reshape(128, 512).astype(BF16), preferred_element_type=F32)
            near, far = total[:ROWS], total[ROWS : 2 * ROWS]
            for direction in ways(g + 2, block):
                inward(direction, g + 2, block).wait_recv()
            if g < 2:
                near = near + zrecv[0, g + 1, :, cols].astype(F32)
                far = far + zrecv[1, g + 1, :, cols].astype(F32)
            elif side == 0:
                near = near + zhalf[:, cols].astype(F32)
            else:
                far = far + zhalf[:, cols].astype(F32)
            zsend[first, :, cols] = near.astype(BF16)
            zsend[second, :, cols] = far.astype(BF16)
            for direction in (0, 1):
                inward(direction, g + 1, block).start()

    def grad_copy(k):
        src, dst = (
            (wgu.at[:, pl.ds(2 * HALF, HALF)], gu_recv.at[0]),
            (wgu.at[:, pl.ds(3 * HALF, HALF)], gu_recv.at[1]),
            (wd.at[pl.ds(HALF, HALF)], d_recv),
        )[k]
        return pltpu.make_async_remote_copy(
            src_ref=src, dst_ref=dst, send_sem=g_s.at[k], recv_sem=g_r.at[k],
            device_id=partner, device_id_type=MESH,
        )

    def gate_up_grads():
        for k in range(3):
            weight_copy(k).wait_send()

        def tile(j, carry):
            rows = pl.ds(pl.multiple_of(j * 256, 256), 256)
            both = lax.dot_general(xs[:, rows], giui[...], TN, preferred_element_type=F32)
            wgu[rows, :] = both.astype(BF16)
            return carry

        lax.fori_loop(0, 8, tile, 0)
        grad_copy(0).start()
        grad_copy(1).start()

    def down_grads():
        def tile_down(j, carry):
            cols = pl.ds(pl.multiple_of(j * 512, 512), 512)
            both = lax.dot_general(hid[...], gs[:, cols], TN, preferred_element_type=F32)
            wd[:, cols] = both.astype(BF16)
            return carry

        lax.fori_loop(0, 4, tile_down, 0)
        grad_copy(2).start()

    def store(k):
        src, dst = (
            (gu_recv.at[0], gate_out), (gu_recv.at[1], up_out), (d_recv, down_out), (result, tok_out)
        )[k]
        return pltpu.make_async_copy(src, dst, store_sem.at[k])

    def add_grads():
        for k in range(2):
            grad_copy(k).wait_recv()

            def tile(j, carry):
                rows = pl.ds(pl.multiple_of(j * 256, 256), 256)
                total = wgu[rows, k * HALF : (k + 1) * HALF].astype(F32) + gu_recv[k, rows, :].astype(F32)
                gu_recv[k, rows, :] = total.astype(BF16)
                return carry

            lax.fori_loop(0, 8, tile, 0)
            store(k).start()
        grad_copy(2).wait_recv()

        def tile_down(j, carry):
            cols = pl.ds(pl.multiple_of(j * 512, 512), 512)
            total = wd[0:HALF, cols].astype(F32) + d_recv[:, cols].astype(F32)
            d_recv[:, cols] = total.astype(BF16)
            return carry

        lax.fori_loop(0, 4, tile_down, 0)
        store(2).start()

    dispatch(3)
    for k in range(3):
        loads[4 + k].wait()
        weight_copy(k).start()
    advance(1, (0, 2))
    near_sel, near_scale = select(1, 2)
    selt[0] = near_sel.T.astype(BF16)
    near_rows = near_sel.astype(BF16)[:, : 2 * ROWS]
    dispatch_near(0, tok, near_rows, None)
    advance(1, (1,))
    dispatch_near(5, grad, near_rows, near_scale)
    advance(2)
    dispatch(1)
    advance(3)
    dispatch(2)
    advance(4)
    dispatch(4)
    selt[3] = select(*PAIRS[3])[0].T.astype(BF16)
    expert_rows(0)
    expert_rows(1)
    expert_rows(2)
    send_back(2)
    expert_rows(3)
    send_back(4)
    send_back(1)
    send_back(0)
    send_back(3)
    gate_up_grads()
    combine_single(1)
    combine(2)
    down_grads()
    combine(1)
    combine(0)
    add_grads()
    combine_single(0)
    for block in (0, 2, 1, 3):
        cols = pl.ds(block * 512, 512)
        for direction in (0, 1):
            inward(direction, 1, block).wait_recv()
        total = own[:, cols] + zrecv[0, 0, :, cols].astype(F32) + zrecv[1, 0, :, cols].astype(F32)
        result[:, cols] = total.astype(BF16)
    store(3).start()

    for h in range(1, 5):
        for direction in (0, 1):
            for piece in pieces(direction, h):
                hop(direction, h, piece).wait_send()
    for k in range(3):
        grad_copy(k).wait_send()
    for h in range(1, 5):
        for block in range(4):
            for direction in ways(h, block):
                inward(direction, h, block).wait_send()

    def drain(i, carry):
        for g in range(6):
            disp(g, i).wait_send()
        for g in range(5):
            ret(g, i).wait_send()
        return carry

    lax.fori_loop(1, 16, drain, 0)
    for k in range(4):
        store(k).wait()


def store_out(*refs):
    sems = refs[8]
    copies = [pltpu.make_async_copy(refs[k], refs[4 + k], sems.at[k]) for k in range(4)]
    for c in copies:
        c.start()
    for c in copies:
        c.wait()


def per_device(tokens, grad_out, expert_ids, gate_probs, gate_weight, up_weight, down_weight):
    anywhere = pl.BlockSpec(memory_space=pl.ANY)
    dma = pltpu.SemaphoreType.DMA
    tok_grad, gate_grad, up_grad, down_grad = pl.pallas_call(
        kernel,
        out_shape=(
            jax.ShapeDtypeStruct((ROWS, D), BF16),
            jax.ShapeDtypeStruct((D, HALF), BF16),
            jax.ShapeDtypeStruct((D, HALF), BF16),
            jax.ShapeDtypeStruct((HALF, D), BF16),
        ),
        in_specs=[pl.BlockSpec(memory_space=pltpu.HBM)] * 7,
        out_specs=[anywhere] * 4,
        scratch_shapes=[
            pltpu.VMEM((TOP, ROWS), jnp.int32),
            pltpu.VMEM((TOP, ROWS), F32),
            pltpu.VMEM((ROWS, D), BF16),
            pltpu.VMEM((REP, ROWS, D), BF16),
            pltpu.VMEM((REP, ROWS, D), BF16),
            pltpu.VMEM((REP, 16, 128), F32),
            pltpu.VMEM((D, 4 * HALF), BF16),
            pltpu.VMEM((2 * HALF, D), BF16),
            pltpu.VMEM((2, 16, 16, D), BF16),
            pltpu.VMEM((2, 16, 16, D), BF16),
            pltpu.VMEM((4, 16, 16, D // 2), BF16),
            pltpu.VMEM((4, 16, 16, D // 2), BF16),
            pltpu.VMEM((GROUPS * 128, D), BF16),
            pltpu.VMEM((GROUPS * 128, D), BF16),
            pltpu.VMEM((GROUPS * 128, 2 * HALF), BF16),
            pltpu.VMEM((GROUPS * 128, 4 * HALF), BF16),
            pltpu.VMEM((3, 16, 16, D // 2), BF16),
            pltpu.VMEM((3, 16, 16, D // 2), BF16),
            pltpu.VMEM((2, 16, 16, D // 4), BF16),
            pltpu.VMEM((2, 16, 16, D // 4), BF16),
            pltpu.VMEM((GROUPS, 128, 128), BF16),
            pltpu.VMEM((REP, ROWS, D), BF16),
            pltpu.VMEM((2, 3, ROWS, D), BF16),
            pltpu.VMEM((ROWS, D), BF16),
            pltpu.VMEM((ROWS, D), F32),
            pltpu.VMEM((2, D, HALF), BF16),
            pltpu.VMEM((HALF, D), BF16),
            dma((7,)),
            dma((4,)),
            dma((2, 4, 3)),
            dma((2, 4, 3)),
            dma((3,)),
            dma((3,)),
            dma((6, 16)),
            dma((6, 16)),
            dma((5, 16)),
            dma((5, 16)),
            dma((2, 4, 4)),
            dma((2, 4, 4)),
            dma((3,)),
            dma((3,)),
        ],
        compiler_params=pltpu.CompilerParams(
            collective_id=0, has_side_effects=True, vmem_limit_bytes=LIMIT * 2**20
        ),
    )(*(
        pltpu.with_memory_space_constraint(x, pltpu.HBM)
        for x in (
            tokens, grad_out, expert_ids.T, gate_probs.T, gate_weight[0], up_weight[0], down_weight[0]
        )
    ))
    outs = (tok_grad, gate_grad, up_grad, down_grad)
    tok_grad, gate_grad, up_grad, down_grad = pl.pallas_call(
        store_out,
        out_shape=tuple(jax.ShapeDtypeStruct(x.shape, x.dtype) for x in outs),
        in_specs=[anywhere] * 4,
        out_specs=[anywhere] * 4,
        scratch_shapes=[dma((4,))],
        compiler_params=pltpu.CompilerParams(vmem_limit_bytes=2**20),
    )(*outs)
    return tok_grad, gate_grad[None], up_grad[None], down_grad[None]


def solution(mesh):
    rows = P(("rep", "exp"), None)
    mats = P(("rep", "exp"), None, None)
    return jax.shard_map(
        per_device,
        mesh=mesh,
        in_specs=(rows, rows, rows, rows, mats, mats, mats),
        out_specs=(rows, mats, mats, mats),
        check_vma=False,
    )
```
